512 devices in a mesh: mp: 32 (over y, x, core), dp: 16 (over z).
Axes of the slice: x: 4, y: 4, z: 16, core: 2. Of those that a mesh axis runs over, the one named last changes fastest.
Arguments:
- momentum: float32 [8192, 14336], P('mp', 'dp'), may hold values from -120 to 120
- gradient: bfloat16 [8192, 14336], P('mp', 'dp'), may hold values from -6 to 6
- weight: bfloat16 [8192, 14336], P('mp', 'dp'), may hold values from -6 to 6
- right_basis: float32 [14336, 256], P('dp'), may hold values from -0.046875 to 0.046875
Outputs:
- new_weight: bfloat16 [8192, 14336], P('mp', 'dp')
- new_momentum: float32 [8192, 14336], P('mp', 'dp')
- new_basis: float32 [14336, 256], P('dp')
The draws below stay inside these ranges and needn't reach their ends.
All inputs are finite; a program needn't handle non-finite values.
Results may differ from the reference program's by a relative error of at most 0.001.
Values sent between devices are 32-bit elements; how exact they have to be, the bound alone decides.
No kernel may reach another device: no remote copies, remote signals or barrier semaphores. Data moves between devices by JAX's collectives and lax.ppermute only.
A program may use at most 64 MiB of HBM per device.

```python
import math
import jax
import jax.numpy as jnp
from jax import lax

ROWS = 8192
COLS = 14336
RANK = 256
ITERS = 2


def draw_momentum(key, part):
    key = jax.random.fold_in(key, 11)
    keys = jax.random.split(key, 3)
    rows_at = jnp.arange(ROWS, dtype=jnp.float32) / ROWS
    cols_at = jnp.arange(COLS, dtype=jnp.float32) / COLS
    row_scale = jnp.exp(jax.random.uniform(keys[1], (ROWS,), jnp.float32, -1.15, 1.15)) * (0.5 + rows_at)
    col_scale = jnp.exp(jax.random.uniform(keys[2], (COLS,), jnp.float32, -1.15, 1.15)) * (0.5 + cols_at)
    noise = jnp.clip(jax.random.normal(keys[0], (ROWS, COLS), jnp.float32), -5.0, 5.0)
    values = noise * row_scale[:, None] * col_scale[None, :]
    return values.astype(jnp.float32)


def level_of(own_key, shape, cuts, smallest, high):
    level = 1.0
    for dim, blocks in cuts:
        heights = jax.random.uniform(jax.random.fold_in(jax.random.fold_in(own_key, 6), dim), (blocks,), jnp.float32, smallest / len(cuts), high / len(cuts))
        level = level * jnp.repeat(jnp.exp(heights), shape[dim] // blocks).reshape((-1,) + (1,) * (len(shape) - 1 - dim))
    return level


def centred(key, extent, width, most, cuts=(), held_as=jnp.bfloat16):
    factor_of = level_of(key, extent, cuts, -0.22, 0.18) if cuts else 1.0
    values = jax.random.normal(key, extent, jnp.float32) * width * factor_of
    return jnp.minimum(jnp.maximum(values, -most), most).astype(held_as)


def setup_inputs(seed: int = 0) -> dict:
    splits = jax.random.split(jax.random.key(seed), 5)
    return {
        "momentum": draw_momentum(jax.random.fold_in(splits[4], 71), 0),
        "gradient": centred(splits[1], (ROWS, COLS), 1.0, 6.0, ((0, 32), (1, 16))),
        "weight": centred(splits[2], (ROWS, COLS), 1.0, 6.0, ((0, 32), (1, 16))),
        "right_basis": centred(splits[3], (COLS, RANK), COLS ** -0.5, 0.046875, ((0, 16),), jnp.float32),
    }


highest = lax.Precision.HIGHEST
retain = 0.95
step_size = 0.5
norm_eps = 1e-06

def reference(momentum, gradient, weight, right_basis):
    buffer = momentum + gradient.astype(jnp.float32)
    basis = right_basis
    left = None
    right = None
    for turn_index in range(ITERS):
        left = jnp.dot(buffer.astype(jnp.float32), basis.astype(jnp.float32), precision=highest, preferred_element_type=jnp.float32)
        gram = lax.dot_general(left.astype(jnp.float32), left.astype(jnp.float32), (((0,), (0,)), ((), ())), precision=highest, preferred_element_type=jnp.float32)
        factor = jnp.linalg.cholesky(gram)
        left = lax.linalg.triangular_solve(factor, left, left_side=False, lower=True, transpose_a=True)
        right = lax.dot_general(buffer.astype(jnp.float32), left.astype(jnp.float32), (((0,), (0,)), ((), ())), precision=highest, preferred_element_type=jnp.float32)
        squares = lax.optimization_barrier(jnp.sum(right * right, axis=0))
        basis = right / (jnp.sqrt(squares) + norm_eps)
    feedback = lax.dot_general(left.astype(jnp.float32), right.astype(jnp.float32), (((1,), (1,)), ((), ())), precision=highest, preferred_element_type=jnp.float32)
    new_momentum = buffer - (1.0 - retain) * feedback
    update = lax.dot_general(left.astype(jnp.float32), basis.astype(jnp.float32), (((1,), (1,)), ((), ())), precision=highest, preferred_element_type=jnp.float32)
    scale = step_size * math.sqrt(ROWS * COLS / RANK)
    new_weight = (weight.astype(jnp.float32) - scale * update).astype(jnp.bfloat16)
    return (new_weight, new_momentum, basis)
```

```python
import math

import jax
import jax.numpy as jnp
from jax import lax
from jax.sharding import PartitionSpec as P

ROWS = 8192
COLS = 14336
RANK = 256
ITERS = 2

highest = lax.Precision.HIGHEST
retain = 0.95
step_size = 0.5
norm_eps = 1e-06

MP = 32
DP = 16
HALF = RANK // 2
SAME_CORE = [[c + 2 * i for i in range(MP // 2)] for c in range(2)]
CORE_PAIRS = [(i, i ^ 1) for i in range(MP)]


def product(first, second):
    return jnp.dot(first, second, precision=highest, preferred_element_type=jnp.float32)


def inner_rows(first, second):
    return lax.dot_general(
        first,
        second,
        (((0,), (0,)), ((), ())),
        precision=highest,
        preferred_element_type=jnp.float32,
    )


def outer_rows(first, second):
    return lax.dot_general(
        first,
        second,
        (((1,), (1,)), ((), ())),
        precision=highest,
        preferred_element_type=jnp.float32,
    )


def scatter_sum(values, axis, count, groups=None):
    rows, columns = values.shape
    parts = lax.all_to_all(values, axis, 0, 0, axis_index_groups=groups, tiled=True)
    return jnp.sum(parts.reshape(count, rows // count, columns), axis=0)


def gather(values, axis, count, groups=None):
    rows, columns = values.shape
    copies = jnp.broadcast_to(values[None], (count, rows, columns))
    return lax.all_to_all(
        copies.reshape(count * rows, columns), axis, 0, 0, axis_index_groups=groups, tiled=True
    )


def sum_over_mp(values):
    core = lax.axis_index("mp") % 2
    first, second = values[:, :HALF], values[:, HALF:]
    own = jnp.where(core == 0, first, second)
    other = jnp.where(core == 0, second, first)
    own = own + lax.ppermute(other, "mp", CORE_PAIRS)
    own = scatter_sum(own, "mp", MP // 2, SAME_CORE)
    own = gather(own, "mp", MP // 2, SAME_CORE)
    other = lax.ppermute(own, "mp", CORE_PAIRS)
    return jnp.concatenate(
        [jnp.where(core == 0, own, other), jnp.where(core == 0, other, own)], axis=1
    )


def scaled_inverse_factor(gram):
    scale = lax.rsqrt(jnp.diagonal(gram))
    factor = jnp.linalg.cholesky(gram * scale[:, None] * scale[None, :])
    inverse = lax.linalg.triangular_solve(
        factor, jnp.eye(RANK, dtype=jnp.float32), left_side=True, lower=True
    )
    return scale, inverse


def body(momentum, gradient, weight, right_basis):
    buffer = momentum + gradient.astype(jnp.float32)
    share = buffer.shape[1]
    own_rows = buffer.shape[0] // DP

    left = scatter_sum(product(buffer, right_basis), "dp", DP)
    left = gather(left, "dp", DP)
    sums = sum_over_mp(jnp.concatenate([inner_rows(buffer, left), inner_rows(left, left)], axis=0))
    scale, inverse = scaled_inverse_factor(sums[share:])
    raw = sums[:share] * scale[None, :]
    left = scatter_sum(product(buffer, raw), "dp", DP)
    right = outer_rows(raw, inverse)
    own_squares = jnp.sum(right * right, axis=0, keepdims=True)
    sent = jnp.concatenate([left, jnp.broadcast_to(own_squares, (8, RANK))], axis=0)
    came = gather(sent, "dp", DP).reshape(DP, own_rows + 8, RANK)
    left = came[:, :own_rows].reshape(DP * own_rows, RANK)
    squares = jnp.sum(came[:, own_rows], axis=0)

    left = outer_rows(left, inverse) / (jnp.sqrt(squares) + norm_eps)[None, :]
    sums = sum_over_mp(jnp.concatenate([inner_rows(buffer, left), inner_rows(left, left)], axis=0))
    scale, inverse = scaled_inverse_factor(sums[share:])
    right = outer_rows(sums[:share] * scale[None, :], inverse)
    left = outer_rows(left * scale[None, :], inverse)
    own_squares = jnp.sum(right * right, axis=0, keepdims=True)
    squares = jnp.sum(gather(own_squares, "dp", DP), axis=0)
    new_momentum = buffer - (1.0 - retain) * outer_rows(left, right)
    basis = right / (jnp.sqrt(squares) + norm_eps)[None, :]
    update = outer_rows(left, basis)
    step = step_size * math.sqrt(ROWS * COLS / RANK)
    new_weight = (weight.astype(jnp.float32) - step * update).astype(jnp.bfloat16)
    return (new_weight, new_momentum, basis)


def solution(mesh):
    in_specs = (P("mp", "dp"), P("mp", "dp"), P("mp", "dp"), P("dp", None))
    out_specs = (P("mp", "dp"), P("mp", "dp"), P("dp", None))
    return jax.shard_map(body, mesh=mesh, in_specs=in_specs, out_specs=out_specs, check_vma=False)
```

```python
import functools
import math

import jax
import jax.numpy as jnp
from jax import lax
from jax.experimental import pallas as pl
from jax.experimental.pallas import tpu as pltpu
from jax.sharding import PartitionSpec as P

ROWS = 8192
COLS = 14336
RANK = 256
ITERS = 2

highest = lax.Precision.HIGHEST
retain = 0.95
step_size = 0.5
norm_eps = 1e-06

MP = 32
DP = 16
HALF = RANK // 2
PANEL = 16
SAME_CORE = [[c + 2 * i for i in range(MP // 2)] for c in range(2)]
CORE_PAIRS = [(i, i ^ 1) for i in range(MP)]


def product(first, second):
    return jnp.dot(first, second, precision=highest, preferred_element_type=jnp.float32)


def inner_rows(first, second):
    return lax.dot_general(
        first,
        second,
        (((0,), (0,)), ((), ())),
        precision=highest,
        preferred_element_type=jnp.float32,
    )


def outer_rows(first, second):
    return lax.dot_general(
        first,
        second,
        (((1,), (1,)), ((), ())),
        precision=highest,
        preferred_element_type=jnp.float32,
    )


def scatter_sum(values, axis, count, groups=None):
    rows, columns = values.shape
    parts = lax.all_to_all(values, axis, 0, 0, axis_index_groups=groups, tiled=True)
    return jnp.sum(parts.reshape(count, rows // count, columns), axis=0)


def gather(values, axis, count, groups=None):
    rows, columns = values.shape
    copies = jnp.broadcast_to(values[None], (count, rows, columns))
    return lax.all_to_all(
        copies.reshape(count * rows, columns), axis, 0, 0, axis_index_groups=groups, tiled=True
    )


def sum_over_mp(values):
    core = lax.axis_index("mp") % 2
    first, second = values[:, :HALF], values[:, HALF:]
    own = jnp.where(core == 0, first, second)
    other = jnp.where(core == 0, second, first)
    own = own + lax.ppermute(other, "mp", CORE_PAIRS)
    own = scatter_sum(own, "mp", MP // 2, SAME_CORE)
    own = gather(own, "mp", MP // 2, SAME_CORE)
    other = lax.ppermute(own, "mp", CORE_PAIRS)
    return jnp.concatenate(
        [jnp.where(core == 0, own, other), jnp.where(core == 0, other, own)], axis=1
    )


def inverse_factor_kernel(gram_ref, out_ref, *, unscale):
    gram = gram_ref[...]
    row = lax.broadcasted_iota(jnp.int32, (RANK, RANK), 0)
    column = lax.broadcasted_iota(jnp.int32, (RANK, RANK), 1)
    diagonal = jnp.where(row == column, gram, 0.0)
    scale_row = lax.rsqrt(jnp.sum(diagonal, axis=0, keepdims=True))
    scale_column = lax.rsqrt(jnp.sum(diagonal, axis=1, keepdims=True))
    rest = gram * scale_column * scale_row
    lane = lax.broadcasted_iota(jnp.int32, (PANEL, RANK), 1)
    place = lax.broadcasted_iota(jnp.int32, (PANEL, RANK), 0)
    short = place[:, :HALF]
    panel, rest = rest[:PANEL], rest[PANEL:]
    for start in range(0, RANK, PANEL):
        own = [
            jnp.broadcast_to(panel[:, start + t : start + t + 1], (PANEL, HALF))
            for t in range(PANEL)
        ]
        inside = (lane >= start) & (lane < start + PANEL)
        panel = jnp.where(inside, jnp.where(lane - start == place, 1.0, 0.0), panel)
        pivots = own[0]
        for t in range(PANEL):
            if t > 0:
                pivots = jnp.where(short == t, own[t], pivots)
            if t < PANEL - 1:
                factor = jnp.where(short > t, own[t] * (1.0 / own[t][t : t + 1]), 0.0)
                for later in range(t + 1, PANEL):
                    own[later] = own[later] - factor * own[later][t : t + 1]
                panel = panel - jnp.concatenate([factor, factor], axis=1) * panel[t : t + 1]
        root = lax.rsqrt(pivots)
        done = panel * jnp.concatenate([root, root], axis=1)
        result = jnp.where(lane < start + PANEL, done, 0.0)
        out_ref[start : start + PANEL, :] = result * scale_row if unscale else result
        if start + PANEL < RANK:
            turned = done.T
            kept = jnp.where(inside, 0.0, 1.0)[:1]
            panel = rest[:PANEL] * kept - product(turned[start + PANEL : start + 2 * PANEL], done)
            if start + 2 * PANEL < RANK:
                rest = rest[PANEL:] * kept - product(turned[start + 2 * PANEL :], done)


def inverse_factor(gram, unscale):
    return pl.pallas_call(
        functools.partial(inverse_factor_kernel, unscale=unscale),
        out_shape=jax.ShapeDtypeStruct((RANK, RANK), jnp.float32),
        cost_estimate=pl.CostEstimate(
            flops=RANK**3 * 12, bytes_accessed=2 * 4 * RANK**2, transcendentals=2 * RANK
        ),
        compiler_params=pltpu.CompilerParams(vmem_limit_bytes=16 * 2**20),
    )(gram)


def diagonal_scale(gram):
    row = lax.broadcasted_iota(jnp.int32, (RANK, RANK), 0)
    column = lax.broadcasted_iota(jnp.int32, (RANK, RANK), 1)
    return lax.rsqrt(jnp.sum(jnp.where(row == column, gram, 0.0), axis=0))


def body(momentum, gradient, weight, right_basis):
    buffer = momentum + gradient.astype(jnp.float32)
    share = buffer.shape[1]
    own_rows = buffer.shape[0] // DP

    left = scatter_sum(product(buffer, right_basis), "dp", DP)
    left = gather(left, "dp", DP)
    sums = sum_over_mp(jnp.concatenate([inner_rows(buffer, left), inner_rows(left, left)], axis=0))
    gram = sums[share:]
    raw = sums[:share] * diagonal_scale(gram)[None, :]
    inverse = inverse_factor(gram, False)
    left = scatter_sum(product(buffer, raw), "dp", DP)
    right = outer_rows(raw, inverse)
    own_squares = jnp.sum(right * right, axis=0, keepdims=True)
    sent = jnp.concatenate([left, jnp.broadcast_to(own_squares, (8, RANK))], axis=0)
    came = gather(sent, "dp", DP).reshape(DP, own_rows + 8, RANK)
    left = came[:, :own_rows].reshape(DP * own_rows, RANK)
    squares = jnp.sum(came[:, own_rows], axis=0)

    left = outer_rows(left, inverse) / (jnp.sqrt(squares) + norm_eps)[None, :]
    sums = sum_over_mp(jnp.concatenate([inner_rows(buffer, left), inner_rows(left, left)], axis=0))
    inverse = inverse_factor(sums[share:], True)
    right = outer_rows(sums[:share], inverse)
    left = outer_rows(left, inverse)
    own_squares = jnp.sum(right * right, axis=0, keepdims=True)
    squares = jnp.sum(gather(own_squares, "dp", DP), axis=0)
    new_momentum = buffer - (1.0 - retain) * outer_rows(left, right)
    basis = right / (jnp.sqrt(squares) + norm_eps)[None, :]
    update = outer_rows(left, basis)
    step = step_size * math.sqrt(ROWS * COLS / RANK)
    new_weight = (weight.astype(jnp.float32) - step * update).astype(jnp.bfloat16)
    return (new_weight, new_momentum, basis)


def solution(mesh):
    in_specs = (P("mp", "dp"), P("mp", "dp"), P("mp", "dp"), P("dp", None))
    out_specs = (P("mp", "dp"), P("mp", "dp"), P("dp", None))
    return jax.shard_map(body, mesh=mesh, in_specs=in_specs, out_specs=out_specs, check_vma=False)
```

```python
import math

import jax
import jax.numpy as jnp
from jax import lax
from jax.experimental import pallas as pl
from jax.experimental.pallas import tpu as pltpu
from jax.sharding import PartitionSpec as P

ROWS = 8192
COLS = 14336
RANK = 256
ITERS = 2

highest = lax.Precision.HIGHEST
retain = 0.95
step_size = 0.5
norm_eps = 1e-06
step = step_size * math.sqrt(ROWS * COLS / RANK)

MP = 32
DP = 16
HALF = RANK // 2
PANEL = 16
OWN_ROWS = ROWS // MP
OWN_COLS = COLS // DP
SAME_CORE = [[c + 2 * i for i in range(MP // 2)] for c in range(2)]
CORE_PAIRS = [(i, i ^ 1) for i in range(MP)]
NEXT_TO = (((1,), (1,)), ((), ()))


def product(first, second):
    return jnp.dot(first, second, precision=highest, preferred_element_type=jnp.float32)


def outer_rows(first, second):
    return lax.dot_general(
        first, second, NEXT_TO, precision=highest, preferred_element_type=jnp.float32
    )


def two_parts(values):
    high = values.astype(jnp.bfloat16)
    return high, (values - high.astype(jnp.float32)).astype(jnp.bfloat16)


def three_parts(values):
    high = values.astype(jnp.bfloat16)
    rest = values - high.astype(jnp.float32)
    middle = rest.astype(jnp.bfloat16)
    return high, middle, (rest - middle.astype(jnp.float32)).astype(jnp.bfloat16)


def product_of_parts(first, second):
    high, low = two_parts(first)
    other_high, other_low = two_parts(second)
    dot = lambda a, b: jnp.dot(a, b, preferred_element_type=jnp.float32)
    return dot(high, other_high) + (dot(high, other_low) + dot(low, other_high))


def on_diagonal():
    row = lax.broadcasted_iota(jnp.int32, (RANK, RANK), 0)
    return row == lax.broadcasted_iota(jnp.int32, (RANK, RANK), 1)


def as_row(column):
    return jnp.sum(jnp.where(on_diagonal(), column, 0.0), axis=0, keepdims=True)


def as_column(row):
    return jnp.sum(jnp.where(on_diagonal(), row, 0.0), axis=1, keepdims=True)


def scales_of(gram):
    diagonal = jnp.where(on_diagonal(), gram, 0.0)
    return (
        lax.rsqrt(jnp.sum(diagonal, axis=1, keepdims=True)),
        lax.rsqrt(jnp.sum(diagonal, axis=0, keepdims=True)),
    )


def write_inverse_factor(rest, out_ref, unscale):
    lane = lax.broadcasted_iota(jnp.int32, (PANEL, RANK), 1)
    place = lax.broadcasted_iota(jnp.int32, (PANEL, RANK), 0)
    short = place[:, :HALF]
    panel, rest = rest[:PANEL], rest[PANEL:]
    for start in range(0, RANK, PANEL):
        own = [
            jnp.broadcast_to(panel[:, start + t : start + t + 1], (PANEL, HALF))
            for t in range(PANEL)
        ]
        inside = (lane >= start) & (lane < start + PANEL)
        panel = jnp.where(inside, jnp.where(lane - start == place, 1.0, 0.0), panel)
        pivots = own[0]
        for t in range(PANEL):
            if t > 0:
                pivots = jnp.where(short == t, own[t], pivots)
            if t < PANEL - 1:
                below = jnp.where(short > t, own[t], 0.0)
                inverse = jnp.broadcast_to(1.0 / own[t][t : t + 1], (PANEL, HALF))
                for later in range(t + 1, PANEL):
                    own[later] = own[later] - (below * own[later][t : t + 1]) * inverse
                factor = below * inverse
                panel = panel - jnp.concatenate([factor, factor], axis=1) * panel[t : t + 1]
        root = lax.rsqrt(pivots)
        done = panel * jnp.concatenate([root, root], axis=1)
        result = jnp.where(lane < start + PANEL, done, 0.0)
        out_ref[start : start + PANEL, :] = result if unscale is None else result * unscale
        end = start + PANEL
        if end < RANK:
            a, b, c = three_parts(done)
            first = jnp.concatenate([a, a, b, b, a, c], axis=0)
            second = jnp.concatenate([a, b, a, b, c, a], axis=0)
            base = 0 if end < HALF else HALF
            taken = lax.dot_general(
                first[:, base:],
                second,
                (((0,), (0,)), ((), ())),
                preferred_element_type=jnp.float32,
            )
            kept = jnp.where(inside, 0.0, 1.0)[:1]
            at = end - base
            panel = rest[:PANEL] * kept - taken[at : at + PANEL]
            if end + PANEL < RANK:
                rest = rest[PANEL:] * kept - taken[at + PANEL :]


def first_kernel(momentum_ref, gradient_ref, basis_ref, buffer_ref, left_ref):
    buffer = momentum_ref[...] + gradient_ref[...].astype(jnp.float32)
    buffer_ref[...] = buffer
    left_ref[...] = product(buffer, basis_ref[...])


def sums_kernel(left_ref, buffer_ref, out_ref):
    left = left_ref[...]
    turned = left.T
    out_ref[:, :OWN_COLS] = product(turned, buffer_ref[...])
    out_ref[:, OWN_COLS:] = product(turned, left)


def next_left_kernel(sums_ref, buffer_ref, out_ref):
    scale, _ = scales_of(sums_ref[:, OWN_COLS:])
    out_ref[...] = outer_rows(buffer_ref[...], sums_ref[:, :OWN_COLS] * scale)


def middle_kernel(sums_ref, inverse_ref, squares_ref):
    gram = sums_ref[:, OWN_COLS:]
    scale, scale_row = scales_of(gram)
    write_inverse_factor(gram * scale * scale_row, inverse_ref, None)
    right = product(inverse_ref[...], sums_ref[:, :OWN_COLS] * scale)
    squares_ref[...] = as_row(jnp.sum(right * right, axis=1, keepdims=True))


def second_left_kernel(raw_ref, inverse_ref, squares_ref, buffer_ref, left_ref, out_ref):
    squares = jnp.sum(squares_ref[...], axis=0, keepdims=True)
    left = outer_rows(raw_ref[...], inverse_ref[...]) / (jnp.sqrt(squares) + norm_eps)
    left_ref[...] = left
    turned = left.T
    out_ref[:, :OWN_COLS] = product(turned, buffer_ref[...])
    out_ref[:, OWN_COLS:] = product(turned, left)


def last_right_kernel(sums_ref, inverse_ref, right_ref, squares_ref):
    gram = sums_ref[:, OWN_COLS:]
    scale, scale_row = scales_of(gram)
    write_inverse_factor(gram * scale * scale_row, inverse_ref, scale_row)
    right = product(inverse_ref[...], sums_ref[:, :OWN_COLS])
    right_ref[...] = right
    squares = as_row(jnp.sum(right * right, axis=1, keepdims=True))
    squares_ref[...] = jnp.broadcast_to(squares[None], (DP, 1, RANK))


def momentum_kernel(raw_ref, inverse_ref, right_ref, buffer_ref, left_ref, out_ref):
    left = outer_rows(raw_ref[...], inverse_ref[...])
    left_ref[...] = left
    out_ref[...] = buffer_ref[...] - (1.0 - retain) * product_of_parts(left, right_ref[...])


def weight_kernel(left_ref, right_ref, squares_ref, weight_ref, basis_ref, out_ref):
    squares = as_column(jnp.sum(squares_ref[...], axis=0))
    basis = right_ref[...] / (jnp.sqrt(squares) + norm_eps)
    basis_ref[...] = basis.T
    update = product_of_parts(left_ref[...], basis)
    out_ref[...] = (weight_ref[...].astype(jnp.float32) - step * update).astype(jnp.bfloat16)


def call(kernel, products, *shapes, dtypes=None, vmem=24):
    dtypes = dtypes or [jnp.float32] * len(shapes)
    out = tuple(jax.ShapeDtypeStruct(s, d) for s, d in zip(shapes, dtypes))
    return pl.pallas_call(
        kernel,
        out_shape=out if len(out) > 1 else out[0],
        cost_estimate=pl.CostEstimate(
            flops=int(products * 12 * RANK * RANK * OWN_COLS),
            bytes_accessed=4 * RANK * OWN_COLS,
            transcendentals=0,
        ),
        compiler_params=pltpu.CompilerParams(vmem_limit_bytes=vmem * 2**20),
    )


def scatter_sum(values, axis, count, groups=None):
    rows, columns = values.shape
    parts = lax.all_to_all(values, axis, 0, 0, axis_index_groups=groups, tiled=True)
    return jnp.sum(parts.reshape(count, rows // count, columns), axis=0)


def gather(values, axis, count, groups=None):
    copies = jnp.broadcast_to(values[None], (count,) + values.shape)
    return lax.all_to_all(copies, axis, 0, 0, axis_index_groups=groups, tiled=True)


def sum_over_mp(values, core):
    halves = values.reshape(2, HALF, values.shape[1])
    own = lax.dynamic_index_in_dim(halves, core, 0, keepdims=False)
    other = lax.dynamic_index_in_dim(halves, 1 - core, 0, keepdims=False)
    own = own + lax.ppermute(other, "mp", CORE_PAIRS)
    own = scatter_sum(own, "mp", MP // 2, SAME_CORE)
    own = gather(own, "mp", MP // 2, SAME_CORE).reshape(HALF, values.shape[1])
    other = lax.ppermute(own, "mp", CORE_PAIRS)
    return jnp.concatenate(
        [jnp.where(core == 0, own, other), jnp.where(core == 0, other, own)], axis=0
    )


def body(momentum, gradient, weight, right_basis):
    square = (RANK, RANK)
    wide = (RANK, OWN_COLS)
    both = (RANK, OWN_COLS + RANK)
    own_rows = OWN_ROWS // DP

    core, momentum = lax.optimization_barrier((lax.axis_index("mp") % 2, momentum))
    buffer, left = call(first_kernel, 1, (OWN_ROWS, OWN_COLS), (OWN_ROWS, RANK), vmem=60)(
        momentum, gradient, right_basis
    )
    left = gather(scatter_sum(left, "dp", DP), "dp", DP).reshape(OWN_ROWS, RANK)
    sums = sum_over_mp(call(sums_kernel, 1.3, both)(left, buffer), core)
    left = scatter_sum(call(next_left_kernel, 1, square)(sums, buffer), "dp", DP)
    inverse, own_squares = call(middle_kernel, 8, square, (1, RANK))(sums)
    sent = jnp.concatenate([left, own_squares], axis=0).reshape(own_rows + 1, 2, HALF)
    came = gather(sent, "dp", DP)
    raw = came[:, :own_rows].reshape(OWN_ROWS, RANK)
    squares = came[:, own_rows].reshape(DP, RANK)

    left, sums = call(second_left_kernel, 1.6, square, both)(raw, inverse, squares, buffer)
    sums = sum_over_mp(sums, core)
    inverse, right, own_squares = call(last_right_kernel, 8, square, wide, (DP, 1, RANK))(sums)
    squares = lax.all_to_all(own_squares, "dp", 0, 0, tiled=True)
    left, new_momentum = call(momentum_kernel, 1, square, (OWN_ROWS, OWN_COLS))(
        left, inverse, right, buffer
    )
    basis, new_weight = call(
        weight_kernel,
        1,
        (OWN_COLS, RANK),
        (OWN_ROWS, OWN_COLS),
        dtypes=[jnp.float32, jnp.bfloat16],
    )(left, right, squares, weight)
    return (new_weight, new_momentum, basis)


def solution(mesh):
    in_specs = (P("mp", "dp"), P("mp", "dp"), P("mp", "dp"), P("dp", None))
    out_specs = (P("mp", "dp"), P("mp", "dp"), P("dp", None))
    return jax.shard_map(body, mesh=mesh, in_specs=in_specs, out_specs=out_specs, check_vma=False)
```

```python
import math

import jax
import jax.numpy as jnp
from jax import lax
from jax.experimental import pallas as pl
from jax.experimental.pallas import tpu as pltpu
from jax.sharding import PartitionSpec as P

ROWS = 8192
COLS = 14336
RANK = 256
ITERS = 2

highest = lax.Precision.HIGHEST
retain = 0.95
step_size = 0.5
norm_eps = 1e-06
step = step_size * math.sqrt(ROWS * COLS / RANK)

MP = 32
DP = 16
HALF = RANK // 2
PANEL = 32
OWN_ROWS = ROWS // MP
OWN_COLS = COLS // DP
SAME_CORE = [[c + 2 * i for i in range(MP // 2)] for c in range(2)]
CORE_PAIRS = [(i, i ^ 1) for i in range(MP)]
NEXT_TO = (((1,), (1,)), ((), ()))


def product(first, second):
    return jnp.dot(first, second, precision=highest, preferred_element_type=jnp.float32)


def outer_rows(first, second):
    return lax.dot_general(
        first, second, NEXT_TO, precision=highest, preferred_element_type=jnp.float32
    )


def two_parts(values):
    high = values.astype(jnp.bfloat16)
    return high, (values - high.astype(jnp.float32)).astype(jnp.bfloat16)


def three_parts(values):
    high = values.astype(jnp.bfloat16)
    rest = values - high.astype(jnp.float32)
    middle = rest.astype(jnp.bfloat16)
    return high, middle, (rest - middle.astype(jnp.float32)).astype(jnp.bfloat16)


def product_of_parts(first, second):
    high, low = two_parts(first)
    other_high, other_low = two_parts(second)
    dot = lambda a, b: jnp.dot(a, b, preferred_element_type=jnp.float32)
    return dot(high, other_high) + (dot(high, other_low) + dot(low, other_high))


def on_diagonal():
    row = lax.broadcasted_iota(jnp.int32, (RANK, RANK), 0)
    return row == lax.broadcasted_iota(jnp.int32, (RANK, RANK), 1)


def as_row(column):
    return jnp.sum(jnp.where(on_diagonal(), column, 0.0), axis=0, keepdims=True)


def as_column(row):
    return jnp.sum(jnp.where(on_diagonal(), row, 0.0), axis=1, keepdims=True)


def scales_of(gram):
    diagonal = jnp.where(on_diagonal(), gram, 0.0)
    return (
        lax.rsqrt(jnp.sum(diagonal, axis=1, keepdims=True)),
        lax.rsqrt(jnp.sum(diagonal, axis=0, keepdims=True)),
    )


def write_inverse_factor(rest, out_ref, unscale):
    lane = lax.broadcasted_iota(jnp.int32, (PANEL, RANK), 1)
    place = lax.broadcasted_iota(jnp.int32, (PANEL, RANK), 0)
    short = lax.broadcasted_iota(jnp.int32, (8, HALF), 0)
    groups = PANEL // 8
    panel, rest = rest[:PANEL], rest[PANEL:]
    for start in range(0, RANK, PANEL):
        own = [
            {
                g: jnp.broadcast_to(
                    panel[8 * g : 8 * g + 8, start + t : start + t + 1], (8, HALF)
                )
                for g in range(t // 8, groups)
            }
            for t in range(PANEL)
        ]
        inside = (lane >= start) & (lane < start + PANEL)
        panel = jnp.where(inside, jnp.where(lane - start == place, 1.0, 0.0), panel)
        rows = [panel[8 * g : 8 * g + 8] for g in range(groups)]
        pivots = [None] * groups
        for t in range(PANEL):
            at, row = divmod(t, 8)
            column = own[t]
            pivots[at] = jnp.where(short == row, column[at], pivots[at]) if row else column[at]
            if t == PANEL - 1:
                break
            inverse = jnp.broadcast_to(1.0 / column[at][row : row + 1], (8, HALF))
            factor = {g: column[g] * inverse for g in range(at, groups)}
            factor[at] = jnp.where(short > row, factor[at], 0.0)
            for later in range(t + 1, PANEL):
                its_group, its_row = divmod(later, 8)
                pivot_row = jnp.broadcast_to(column[its_group][its_row : its_row + 1], (8, HALF))
                for g in range(its_group, groups):
                    own[later][g] = own[later][g] - factor[g] * pivot_row
            pivot_row = rows[at][row : row + 1]
            for g in range(at, groups):
                rows[g] = rows[g] - jnp.concatenate([factor[g]] * 2, axis=1) * pivot_row
        for g in range(groups):
            root = lax.rsqrt(pivots[g])
            rows[g] = rows[g] * jnp.concatenate([root, root], axis=1)
        done = jnp.concatenate(rows, axis=0)
        result = jnp.where(lane < start + PANEL, done, 0.0)
        out_ref[start : start + PANEL, :] = result if unscale is None else result * unscale
        end = start + PANEL
        if end < RANK:
            a, b, c = three_parts(done)
            first = jnp.concatenate([a, a, b, b, a, c], axis=0)
            second = jnp.concatenate([a, b, a, b, c, a], axis=0)
            base = 0 if end < HALF else HALF
            taken = lax.dot_general(
                first[:, base:],
                second,
                (((0,), (0,)), ((), ())),
                preferred_element_type=jnp.float32,
            )
            kept = jnp.where(inside, 0.0, 1.0)[:1]
            at = end - base
            panel = rest[:PANEL] * kept - taken[at : at + PANEL]
            if end + PANEL < RANK:
                rest = rest[PANEL:] * kept - taken[at + PANEL :]


def buffer_of(momentum_ref, gradient_ref):
    return momentum_ref[...] + gradient_ref[...].astype(jnp.float32)


def first_kernel(momentum_ref, gradient_ref, basis_ref, left_ref):
    left_ref[...] = product(buffer_of(momentum_ref, gradient_ref), basis_ref[...])


def sums_kernel(left_ref, momentum_ref, gradient_ref, out_ref):
    left = left_ref[...]
    turned = left.T
    out_ref[:, :OWN_COLS] = product(turned, buffer_of(momentum_ref, gradient_ref))
    out_ref[:, OWN_COLS:] = product(turned, left)


def next_left_kernel(sums_ref, momentum_ref, gradient_ref, out_ref):
    scale, _ = scales_of(sums_ref[:, OWN_COLS:])
    buffer = buffer_of(momentum_ref, gradient_ref)
    out_ref[...] = outer_rows(buffer, sums_ref[:, :OWN_COLS] * scale)


def middle_kernel(sums_ref, inverse_ref, squares_ref):
    gram = sums_ref[:, OWN_COLS:]
    scale, scale_row = scales_of(gram)
    write_inverse_factor(gram * scale * scale_row, inverse_ref, None)
    right = product(inverse_ref[...], sums_ref[:, :OWN_COLS] * scale)
    squares_ref[...] = as_row(jnp.sum(right * right, axis=1, keepdims=True))


def second_left_kernel(
    raw_ref, inverse_ref, squares_ref, momentum_ref, gradient_ref, left_ref, out_ref
):
    squares = jnp.sum(squares_ref[...], axis=0, keepdims=True)
    left = outer_rows(raw_ref[...], inverse_ref[...]) / (jnp.sqrt(squares) + norm_eps)
    left_ref[...] = left
    turned = left.T
    out_ref[:, :OWN_COLS] = product(turned, buffer_of(momentum_ref, gradient_ref))
    out_ref[:, OWN_COLS:] = product(turned, left)


def last_right_kernel(sums_ref, inverse_ref, right_ref, squares_ref):
    gram = sums_ref[:, OWN_COLS:]
    scale, scale_row = scales_of(gram)
    write_inverse_factor(gram * scale * scale_row, inverse_ref, scale_row)
    right = product(inverse_ref[...], sums_ref[:, :OWN_COLS])
    right_ref[...] = right
    squares = as_row(jnp.sum(right * right, axis=1, keepdims=True))
    squares_ref[...] = jnp.broadcast_to(squares[None], (DP, 1, RANK))


def momentum_kernel(
    raw_ref, inverse_ref, right_ref, momentum_ref, gradient_ref, left_ref, out_ref
):
    left = outer_rows(raw_ref[...], inverse_ref[...])
    left_ref[...] = left
    buffer = buffer_of(momentum_ref, gradient_ref)
    out_ref[...] = buffer - (1.0 - retain) * product_of_parts(left, right_ref[...])


def weight_kernel(
    left_ref, right_ref, squares_ref, weight_ref, basis_out, weight_out, own_b, own_w, done
):
    squares = as_column(jnp.sum(squares_ref[...], axis=0))
    basis = right_ref[...] / (jnp.sqrt(squares) + norm_eps)
    own_b[...] = basis.T
    first = pltpu.make_async_copy(own_b, basis_out, done.at[0])
    first.start()
    update = product_of_parts(left_ref[...], basis)
    own_w[...] = (weight_ref[...].astype(jnp.float32) - step * update).astype(jnp.bfloat16)
    second = pltpu.make_async_copy(own_w, weight_out, done.at[1])
    second.start()
    first.wait()
    second.wait()


def call(kernel, products, *shapes, **options):
    vmem = options.pop("vmem", 24)
    dtypes = options.pop("dtypes", [jnp.float32] * len(shapes))
    out = tuple(jax.ShapeDtypeStruct(s, d) for s, d in zip(shapes, dtypes))
    return pl.pallas_call(
        kernel,
        out_shape=out if len(out) > 1 else out[0],
        cost_estimate=pl.CostEstimate(
            flops=int(products * 12 * RANK * RANK * OWN_COLS),
            bytes_accessed=4 * RANK * OWN_COLS,
            transcendentals=0,
        ),
        compiler_params=pltpu.CompilerParams(vmem_limit_bytes=vmem * 2**20),
        **options,
    )


def scatter_sum(values, axis, count, groups=None):
    rows, columns = values.shape
    parts = lax.all_to_all(values, axis, 0, 0, axis_index_groups=groups, tiled=True)
    return jnp.sum(parts.reshape(count, rows // count, columns), axis=0)


def gather(values, axis, count, groups=None):
    copies = jnp.broadcast_to(values[None], (count,) + values.shape)
    return lax.all_to_all(copies, axis, 0, 0, axis_index_groups=groups, tiled=True)


def sum_over_mp(values, first_core, own_start, other_start):
    width = values.shape[1]
    zero = own_start * 0
    own = lax.dynamic_slice(values, (own_start, zero), (HALF, width))
    other = lax.dynamic_slice(values, (other_start, zero), (HALF, width))
    own = own + lax.ppermute(other, "mp", CORE_PAIRS)
    own = scatter_sum(own, "mp", MP // 2, SAME_CORE)
    own = gather(own, "mp", MP // 2, SAME_CORE).reshape(HALF, width)
    other = lax.ppermute(own, "mp", CORE_PAIRS)
    return jnp.concatenate(
        [jnp.where(first_core, own, other), jnp.where(first_core, other, own)], axis=0
    )


def body(momentum, gradient, weight, right_basis):
    square = (RANK, RANK)
    wide = (RANK, OWN_COLS)
    both = (RANK, OWN_COLS + RANK)
    block = (OWN_ROWS, OWN_COLS)
    own_rows = OWN_ROWS // DP
    anywhere = pl.BlockSpec(memory_space=pl.ANY)

    core = (lax.axis_index("mp") % 2).astype(jnp.uint32)
    *halves, right_basis = lax.optimization_barrier(
        (core == 0, core * HALF, HALF - core * HALF, right_basis)
    )

    left = call(first_kernel, 1, (OWN_ROWS, RANK), vmem=60)(momentum, gradient, right_basis)
    left = gather(scatter_sum(left, "dp", DP), "dp", DP).reshape(OWN_ROWS, RANK)
    sums = sum_over_mp(call(sums_kernel, 1.3, both)(left, momentum, gradient), *halves)
    left = call(next_left_kernel, 1, square)(sums, momentum, gradient)
    left = scatter_sum(left, "dp", DP)
    inverse, own_squares = call(middle_kernel, 8, square, (1, RANK))(sums)
    sent = jnp.concatenate([left, own_squares], axis=0).reshape(own_rows + 1, 2, HALF)
    came = gather(sent, "dp", DP)
    raw = came[:, :own_rows].reshape(OWN_ROWS, RANK)
    squares = came[:, own_rows].reshape(DP, RANK)

    left, sums = call(second_left_kernel, 1.6, square, both)(
        raw, inverse, squares, momentum, gradient
    )
    sums = sum_over_mp(sums, *halves)
    inverse, right, own_squares = call(last_right_kernel, 8, square, wide, (DP, 1, RANK))(sums)
    squares = lax.all_to_all(own_squares, "dp", 0, 0, tiled=True)
    left, new_momentum = call(momentum_kernel, 1, square, block)(
        left, inverse, right, momentum, gradient
    )
    basis, new_weight = call(
        weight_kernel,
        1,
        (OWN_COLS, RANK),
        block,
        dtypes=[jnp.float32, jnp.bfloat16],
        out_specs=(anywhere, anywhere),
        scratch_shapes=[
            pltpu.VMEM((OWN_COLS, RANK), jnp.float32),
            pltpu.VMEM(block, jnp.bfloat16),
            pltpu.SemaphoreType.DMA((2,)),
        ],
    )(left, right, squares, weight)
    return (new_weight, new_momentum, basis)


def solution(mesh):
    in_specs = (P("mp", "dp"), P("mp", "dp"), P("mp", "dp"), P("dp", None))
    out_specs = (P("mp", "dp"), P("mp", "dp"), P("dp", None))
    return jax.shard_map(body, mesh=mesh, in_specs=in_specs, out_specs=out_specs, check_vma=False)
```

```python
import math

import jax
import jax.numpy as jnp
from jax import lax
from jax.experimental import pallas as pl
from jax.experimental.pallas import tpu as pltpu
from jax.sharding import PartitionSpec as P

ROWS = 8192
COLS = 14336
RANK = 256
ITERS = 2

highest = lax.Precision.HIGHEST
retain = 0.95
step_size = 0.5
norm_eps = 1e-06
step = step_size * math.sqrt(ROWS * COLS / RANK)

MP = 32
DP = 16
HALF = RANK // 2
PANEL = 16
OWN_ROWS = ROWS // MP
OWN_COLS = COLS // DP
SAME_CORE = [[c + 2 * i for i in range(MP // 2)] for c in range(2)]
CORE_PAIRS = [(i, i ^ 1) for i in range(MP)]
NEXT_TO = (((1,), (1,)), ((), ()))


def product(first, second):
    return jnp.dot(first, second, precision=highest, preferred_element_type=jnp.float32)


def outer_rows(first, second):
    return lax.dot_general(
        first, second, NEXT_TO, precision=highest, preferred_element_type=jnp.float32
    )


def two_parts(values):
    high = values.astype(jnp.bfloat16)
    return high, (values - high.astype(jnp.float32)).astype(jnp.bfloat16)


def three_parts(values):
    high = values.astype(jnp.bfloat16)
    rest = values - high.astype(jnp.float32)
    middle = rest.astype(jnp.bfloat16)
    return high, middle, (rest - middle.astype(jnp.float32)).astype(jnp.bfloat16)


def product_of_parts(first, second):
    high, low = two_parts(first)
    other_high, other_low = two_parts(second)
    dot = lambda a, b: jnp.dot(a, b, preferred_element_type=jnp.float32)
    return dot(high, other_high) + (dot(high, other_low) + dot(low, other_high))


def on_diagonal():
    row = lax.broadcasted_iota(jnp.int32, (RANK, RANK), 0)
    return row == lax.broadcasted_iota(jnp.int32, (RANK, RANK), 1)


def as_row(column):
    return jnp.sum(jnp.where(on_diagonal(), column, 0.0), axis=0, keepdims=True)


def as_column(row):
    return jnp.sum(jnp.where(on_diagonal(), row, 0.0), axis=1, keepdims=True)


def scales_of(gram):
    diagonal = jnp.where(on_diagonal(), gram, 0.0)
    return (
        lax.rsqrt(jnp.sum(diagonal, axis=1, keepdims=True)),
        lax.rsqrt(jnp.sum(diagonal, axis=0, keepdims=True)),
    )


def spread(row):
    return jnp.broadcast_to(row, (8, HALF))


def doubled(values):
    return jnp.concatenate([values, values], axis=1)


def write_inverse_factor(rest, out_ref, unscale):
    lane = lax.broadcasted_iota(jnp.int32, (PANEL, RANK), 1)
    place = lax.broadcasted_iota(jnp.int32, (PANEL, RANK), 0)
    short = lax.broadcasted_iota(jnp.int32, (8, HALF), 0)
    groups = PANEL // 8
    panel, rest = rest[:PANEL], rest[PANEL:]
    for start in range(0, RANK, PANEL):
        own = [
            {
                g: jnp.broadcast_to(
                    panel[8 * g : 8 * g + 8, start + t : start + t + 1], (8, HALF)
                )
                for g in range(t // 8, groups)
            }
            for t in range(PANEL)
        ]
        inside = (lane >= start) & (lane < start + PANEL)
        panel = jnp.where(inside, jnp.where(lane - start == place, 1.0, 0.0), panel)
        rows = [panel[8 * g : 8 * g + 8] for g in range(groups)]
        pivots = [None] * groups
        for t in range(0, PANEL, 2):
            at, row = divmod(t, 8)
            one, two = own[t], own[t + 1]
            p = spread(one[at][row : row + 1])
            r = spread(one[at][row + 1 : row + 2])
            minor = p * spread(two[at][row + 1 : row + 2]) - r * r
            over_p = 1.0 / p
            over_q = p * (1.0 / minor)
            ratio = r * over_p
            pair = jnp.where(short == row, p, minor * over_p)
            pivots[at] = jnp.where(short >= row, pair, pivots[at]) if row else pair
            two = {g: two[g] - one[g] * ratio for g in range(at, groups)}
            by_one = {g: one[g] * over_p for g in range(at, groups)}
            by_two = {g: two[g] * over_q for g in range(at, groups)}
            by_one[at] = jnp.where(short > row, by_one[at], 0.0)
            by_two[at] = jnp.where(short > row + 1, by_two[at], 0.0)
            for later in range(t + 2, PANEL):
                its_group, its_row = divmod(later, 8)
                from_one = spread(one[its_group][its_row : its_row + 1])
                from_two = spread(two[its_group][its_row : its_row + 1])
                for g in range(its_group, groups):
                    own[later][g] = own[later][g] - by_one[g] * from_one - by_two[g] * from_two
            first = rows[at][row : row + 1]
            second = rows[at][row + 1 : row + 2] - doubled(ratio[:1]) * first
            for g in range(at, groups):
                rows[g] = rows[g] - doubled(by_one[g]) * first - doubled(by_two[g]) * second
        for g in range(groups):
            root = lax.rsqrt(pivots[g])
            rows[g] = rows[g] * doubled(root)
        done = jnp.concatenate(rows, axis=0)
        result = jnp.where(lane < start + PANEL, done, 0.0)
        out_ref[start : start + PANEL, :] = result if unscale is None else result * unscale
        end = start + PANEL
        if end < RANK:
            a, b, c = three_parts(done)
            first = jnp.concatenate([a, a, b, b, a, c], axis=0)
            second = jnp.concatenate([a, b, a, b, c, a], axis=0)
            base = 0 if end < HALF else HALF
            taken = lax.dot_general(
                first[:, base:],
                second,
                (((0,), (0,)), ((), ())),
                preferred_element_type=jnp.float32,
            )
            kept = jnp.where(inside, 0.0, 1.0)[:1]
            at = end - base
            panel = rest[:PANEL] * kept - taken[at : at + PANEL]
            if end + PANEL < RANK:
                rest = rest[PANEL:] * kept - taken[at + PANEL :]


def first_kernel(momentum_ref, gradient_ref, basis_ref, buffer_ref, left_ref):
    buffer = momentum_ref[...] + gradient_ref[...].astype(jnp.float32)
    buffer_ref[...] = buffer
    left_ref[...] = product(buffer, basis_ref[...])


def sums_kernel(left_ref, buffer_ref, out_ref):
    left = left_ref[...]
    turned = left.T
    out_ref[:, :OWN_COLS] = product(turned, buffer_ref[...])
    out_ref[:, OWN_COLS:] = product(turned, left)


def next_left_kernel(core_ref, half_ref, buffer_ref, other_ref, out_ref):
    core = core_ref[0]
    row = lax.broadcasted_iota(jnp.int32, (HALF, RANK), 0)
    column = lax.broadcasted_iota(jnp.int32, (HALF, RANK), 1)
    diagonal = jnp.where(column == row + core * HALF, half_ref[:, OWN_COLS:], 0.0)
    scale = lax.rsqrt(jnp.sum(diagonal, axis=1, keepdims=True))
    right = half_ref[:, :OWN_COLS] * scale
    mine = pl.ds(pl.multiple_of(core * OWN_ROWS, OWN_ROWS), OWN_ROWS)
    its = pl.ds(pl.multiple_of((1 - core) * OWN_ROWS, OWN_ROWS), OWN_ROWS)
    out_ref[mine, :] = outer_rows(buffer_ref[...], right)
    out_ref[its, :] = outer_rows(other_ref[...], right)


def middle_kernel(sums_ref, inverse_ref, squares_ref):
    gram = sums_ref[:, OWN_COLS:]
    scale, scale_row = scales_of(gram)
    write_inverse_factor(gram * scale * scale_row, inverse_ref, None)
    right = product(inverse_ref[...], sums_ref[:, :OWN_COLS] * scale)
    squares_ref[...] = as_row(jnp.sum(right * right, axis=1, keepdims=True))


def second_left_kernel(
    core_ref, raw_ref, raw_other_ref, inverse_ref, squares_ref, buffer_ref, other_ref, left_ref, out_ref
):
    first_core = core_ref[0] == 0
    pick = lambda a, b: jnp.where(first_core, a, b)
    mine, its = raw_ref[...], raw_other_ref[...]
    raw = jnp.concatenate([pick(mine, its), pick(its, mine)], axis=1)
    squares = jnp.sum(squares_ref[...], axis=0, keepdims=True)
    left = outer_rows(raw, inverse_ref[...]) / (jnp.sqrt(squares) + norm_eps)
    left_ref[...] = pick(left[:OWN_ROWS], left[OWN_ROWS:])
    turned = pick(left[:, :HALF], left[:, HALF:]).T
    early, late = turned[:, :OWN_ROWS], turned[:, OWN_ROWS:]
    out_ref[:, :OWN_COLS] = product(pick(early, late), buffer_ref[...]) + product(
        pick(late, early), other_ref[...]
    )
    out_ref[:, OWN_COLS:] = product(turned, left)


def last_right_kernel(sums_ref, inverse_ref, right_ref, squares_ref):
    gram = sums_ref[:, OWN_COLS:]
    scale, scale_row = scales_of(gram)
    write_inverse_factor(gram * scale * scale_row, inverse_ref, scale_row)
    right = product(inverse_ref[...], sums_ref[:, :OWN_COLS])
    right_ref[...] = right
    squares = as_row(jnp.sum(right * right, axis=1, keepdims=True))
    squares_ref[...] = jnp.broadcast_to(squares[None], (DP, 1, RANK))


def momentum_kernel(raw_ref, inverse_ref, right_ref, buffer_ref, left_ref, out_ref):
    left = outer_rows(raw_ref[...], inverse_ref[...])
    left_ref[...] = left
    out_ref[...] = buffer_ref[...] - (1.0 - retain) * product_of_parts(left, right_ref[...])


def weight_kernel(
    left_ref, right_ref, squares_ref, weight_ref, basis_out, weight_out, own_b, own_w, done
):
    squares = as_column(jnp.sum(squares_ref[...], axis=0))
    basis = right_ref[...] / (jnp.sqrt(squares) + norm_eps)
    own_b[...] = basis.T
    first = pltpu.make_async_copy(own_b, basis_out, done.at[0])
    first.start()
    update = product_of_parts(left_ref[...], basis)
    own_w[...] = (weight_ref[...].astype(jnp.float32) - step * update).astype(jnp.bfloat16)
    second = pltpu.make_async_copy(own_w, weight_out, done.at[1])
    second.start()
    first.wait()
    second.wait()


def call(kernel, products, *shapes, **options):
    vmem = options.pop("vmem", 24)
    dtypes = options.pop("dtypes", [jnp.float32] * len(shapes))
    out = tuple(jax.ShapeDtypeStruct(s, d) for s, d in zip(shapes, dtypes))
    return pl.pallas_call(
        kernel,
        out_shape=out if len(out) > 1 else out[0],
        cost_estimate=pl.CostEstimate(
            flops=int(products * 12 * RANK * RANK * OWN_COLS),
            bytes_accessed=4 * RANK * OWN_COLS,
            transcendentals=0,
        ),
        compiler_params=pltpu.CompilerParams(vmem_limit_bytes=vmem * 2**20),
        **options,
    )


def scatter_sum(values, axis, count, groups=None):
    rows, columns = values.shape
    parts = lax.all_to_all(values, axis, 0, 0, axis_index_groups=groups, tiled=True)
    return jnp.sum(parts.reshape(count, rows // count, columns), axis=0)


def gather(values, axis, count, groups=None):
    copies = jnp.broadcast_to(values[None], (count,) + values.shape)
    return lax.all_to_all(copies, axis, 0, 0, axis_index_groups=groups, tiled=True)


def sum_over_chips(values):
    own = scatter_sum(values, "mp", MP // 2, SAME_CORE)
    return gather(own, "mp", MP // 2, SAME_CORE).reshape(values.shape)


def with_other_core(values):
    return lax.ppermute(values, "mp", CORE_PAIRS)


def joined(half, first_core):
    other = with_other_core(half)
    return jnp.concatenate(
        [jnp.where(first_core, half, other), jnp.where(first_core, other, half)], axis=0
    )


def body(momentum, gradient, weight, right_basis):
    square = (RANK, RANK)
    wide = (RANK, OWN_COLS)
    width = OWN_COLS + RANK
    block = (OWN_ROWS, OWN_COLS)
    anywhere = pl.BlockSpec(memory_space=pl.ANY)
    scalar = pl.BlockSpec(memory_space=pltpu.SMEM)
    vector = pl.BlockSpec(memory_space=pltpu.VMEM)

    core = (lax.axis_index("mp") % 2).astype(jnp.uint32)
    first_core, own_start, other_start, zero, core, right_basis = lax.optimization_barrier(
        (
            core == 0,
            core * HALF,
            HALF - core * HALF,
            core * 0,
            core.astype(jnp.int32).reshape(1),
            right_basis,
        )
    )

    buffer, left = call(first_kernel, 1, block, (OWN_ROWS, RANK), vmem=60)(
        momentum, gradient, right_basis
    )
    buffer_other = with_other_core(buffer)
    left = gather(scatter_sum(left, "dp", DP), "dp", DP).reshape(OWN_ROWS, RANK)
    sums = call(sums_kernel, 1.3, (RANK, width))(left, buffer)
    half = lax.dynamic_slice(sums, (own_start, zero), (HALF, width))
    other = lax.dynamic_slice(sums, (other_start, zero), (HALF, width))
    half = scatter_sum(half + with_other_core(other), "mp", MP // 2, SAME_CORE)
    half, buffer_other = lax.optimization_barrier((half, buffer_other))
    half = gather(half, "mp", MP // 2, SAME_CORE).reshape(HALF, width)
    raw = call(
        next_left_kernel, 1, (2 * OWN_ROWS, HALF), in_specs=[scalar, vector, vector, vector]
    )(core, half, buffer, buffer_other)
    raw = scatter_sum(raw, "dp", DP)
    inverse, own_squares = call(middle_kernel, 8, square, (1, RANK))(joined(half, first_core))
    shared = 2 * OWN_ROWS // DP
    sent = [raw.reshape(shared // 2, 2, HALF), own_squares.reshape(1, 2, HALF)]
    came = gather(jnp.concatenate(sent, axis=0), "dp", DP)
    raw = came[:, : shared // 2].reshape(2 * OWN_ROWS, HALF)
    squares = came[:, shared // 2].reshape(DP, RANK)

    left, half = call(
        second_left_kernel, 1.6, square, (HALF, width), in_specs=[scalar] + [vector] * 6
    )(core, raw, with_other_core(raw), inverse, squares, buffer, buffer_other)
    sums = joined(sum_over_chips(half), first_core)
    inverse, right, own_squares = call(last_right_kernel, 8, square, wide, (DP, 1, RANK))(sums)
    squares = lax.all_to_all(own_squares, "dp", 0, 0, tiled=True)
    left, new_momentum = call(momentum_kernel, 1, square, block)(left, inverse, right, buffer)
    basis, new_weight = call(
        weight_kernel,
        1,
        (OWN_COLS, RANK),
        block,
        dtypes=[jnp.float32, jnp.bfloat16],
        out_specs=(anywhere, anywhere),
        scratch_shapes=[
            pltpu.VMEM((OWN_COLS, RANK), jnp.float32),
            pltpu.VMEM(block, jnp.bfloat16),
            pltpu.SemaphoreType.DMA((2,)),
        ],
    )(left, right, squares, weight)
    return (new_weight, new_momentum, basis)


def solution(mesh):
    in_specs = (P("mp", "dp"), P("mp", "dp"), P("mp", "dp"), P("dp", None))
    out_specs = (P("mp", "dp"), P("mp", "dp"), P("dp", None))
    return jax.shard_map(body, mesh=mesh, in_specs=in_specs, out_specs=out_specs, check_vma=False)
```

```python
import math

import jax
import jax.numpy as jnp
from jax import lax
from jax.experimental import pallas as pl
from jax.experimental.pallas import tpu as pltpu
from jax.sharding import PartitionSpec as P

ROWS = 8192
COLS = 14336
RANK = 256
ITERS = 2

highest = lax.Precision.HIGHEST
retain = 0.95
step_size = 0.5
norm_eps = 1e-06
step = step_size * math.sqrt(ROWS * COLS / RANK)

MP = 32
DP = 16
HALF = RANK // 2
PANEL = 16
OWN_ROWS = ROWS // MP
OWN_COLS = COLS // DP
SAME_CORE = [[c + 2 * i for i in range(MP // 2)] for c in range(2)]
CORE_PAIRS = [(i, i ^ 1) for i in range(MP)]
NEXT_TO = (((1,), (1,)), ((), ()))


def product(first, second):
    return jnp.dot(first, second, precision=highest, preferred_element_type=jnp.float32)


def outer_rows(first, second):
    return lax.dot_general(
        first, second, NEXT_TO, precision=highest, preferred_element_type=jnp.float32
    )


def two_parts(values):
    high = values.astype(jnp.bfloat16)
    return high, (values - high.astype(jnp.float32)).astype(jnp.bfloat16)


def three_parts(values):
    high = values.astype(jnp.bfloat16)
    rest = values - high.astype(jnp.float32)
    middle = rest.astype(jnp.bfloat16)
    return high, middle, (rest - middle.astype(jnp.float32)).astype(jnp.bfloat16)


def product_of_parts(first, second):
    high, low = two_parts(first)
    other_high, other_low = two_parts(second)
    dot = lambda a, b: jnp.dot(a, b, preferred_element_type=jnp.float32)
    return dot(high, other_high) + (dot(high, other_low) + dot(low, other_high))


def outer_rows_paired(first, second):
    rows = second.shape[0]
    a, b, c = three_parts(first)
    high, middle, low = three_parts(second)
    dot = lambda x, y: lax.dot_general(x, y, NEXT_TO, preferred_element_type=jnp.float32)
    pair = jnp.concatenate([high, middle], axis=0)
    by_a, by_b = dot(a, pair), dot(b, pair)
    small = by_b[:, rows:] + dot(a, low) + dot(c, high)
    return by_a[:, :rows] + (by_a[:, rows:] + by_b[:, :rows] + small)


def on_diagonal():
    row = lax.broadcasted_iota(jnp.int32, (RANK, RANK), 0)
    return row == lax.broadcasted_iota(jnp.int32, (RANK, RANK), 1)


def as_row(column):
    return jnp.sum(jnp.where(on_diagonal(), column, 0.0), axis=0, keepdims=True)


def as_column(row):
    return jnp.sum(jnp.where(on_diagonal(), row, 0.0), axis=1, keepdims=True)


def scales_of(gram):
    diagonal = jnp.where(on_diagonal(), gram, 0.0)
    return (
        lax.rsqrt(jnp.sum(diagonal, axis=1, keepdims=True)),
        lax.rsqrt(jnp.sum(diagonal, axis=0, keepdims=True)),
    )


def spread(row):
    return jnp.broadcast_to(row, (8, HALF))


def doubled(values):
    return jnp.concatenate([values, values], axis=1)


def write_inverse_factor(rest, out_ref, unscale):
    lane = lax.broadcasted_iota(jnp.int32, (PANEL, RANK), 1)
    place = lax.broadcasted_iota(jnp.int32, (PANEL, RANK), 0)
    short = lax.broadcasted_iota(jnp.int32, (8, HALF), 0)
    groups = PANEL // 8
    panel, rest = rest[:PANEL], rest[PANEL:]
    for start in range(0, RANK, PANEL):
        own = [
            {
                g: jnp.broadcast_to(
                    panel[8 * g : 8 * g + 8, start + t : start + t + 1], (8, HALF)
                )
                for g in range(t // 8, groups)
            }
            for t in range(PANEL)
        ]
        inside = (lane >= start) & (lane < start + PANEL)
        panel = jnp.where(inside, jnp.where(lane - start == place, 1.0, 0.0), panel)
        rows = [panel[8 * g : 8 * g + 8] for g in range(groups)]
        pivots = [None] * groups
        for t in range(0, PANEL, 2):
            at, row = divmod(t, 8)
            one, two = own[t], own[t + 1]
            p = spread(one[at][row : row + 1])
            r = spread(one[at][row + 1 : row + 2])
            minor = p * spread(two[at][row + 1 : row + 2]) - r * r
            over_p = 1.0 / p
            over_q = p * (1.0 / minor)
            ratio = r * over_p
            pair = jnp.where(short == row, p, minor * over_p)
            pivots[at] = jnp.where(short >= row, pair, pivots[at]) if row else pair
            two = {g: two[g] - one[g] * ratio for g in range(at, groups)}
            by_one = {g: one[g] * over_p for g in range(at, groups)}
            by_two = {g: two[g] * over_q for g in range(at, groups)}
            by_one[at] = jnp.where(short > row, by_one[at], 0.0)
            by_two[at] = jnp.where(short > row + 1, by_two[at], 0.0)
            for later in range(t + 2, PANEL):
                its_group, its_row = divmod(later, 8)
                from_one = spread(one[its_group][its_row : its_row + 1])
                from_two = spread(two[its_group][its_row : its_row + 1])
                for g in range(its_group, groups):
                    own[later][g] = own[later][g] - by_one[g] * from_one - by_two[g] * from_two
            first = rows[at][row : row + 1]
            second = rows[at][row + 1 : row + 2] - doubled(ratio[:1]) * first
            for g in range(at, groups):
                rows[g] = rows[g] - doubled(by_one[g]) * first - doubled(by_two[g]) * second
        for g in range(groups):
            root = lax.rsqrt(pivots[g])
            rows[g] = rows[g] * doubled(root)
        done = jnp.concatenate(rows, axis=0)
        result = jnp.where(lane < start + PANEL, done, 0.0)
        out_ref[start : start + PANEL, :] = result if unscale is None else result * unscale
        end = start + PANEL
        if end < RANK:
            a, b, c = three_parts(done)
            first = jnp.concatenate([a, a, b, b, a, c], axis=0)
            second = jnp.concatenate([a, b, a, b, c, a], axis=0)
            base = 0 if end < HALF else HALF
            taken = lax.dot_general(
                first[:, base:],
                second,
                (((0,), (0,)), ((), ())),
                preferred_element_type=jnp.float32,
            )
            kept = jnp.where(inside, 0.0, 1.0)[:1]
            at = end - base
            panel = rest[:PANEL] * kept - taken[at : at + PANEL]
            if end + PANEL < RANK:
                rest = rest[PANEL:] * kept - taken[at + PANEL :]


def first_kernel(momentum_ref, gradient_ref, basis_ref, buffer_ref, left_ref):
    buffer = momentum_ref[...] + gradient_ref[...].astype(jnp.float32)
    buffer_ref[...] = buffer
    left_ref[...] = product(buffer, basis_ref[...])


def sums_kernel(left_ref, buffer_ref, out_ref):
    left = left_ref[...]
    turned = left.T
    out_ref[:, :OWN_COLS] = product(turned, buffer_ref[...])
    out_ref[:, OWN_COLS:] = product(turned, left)


def next_left_kernel(core_ref, half_ref, buffer_ref, other_ref, out_ref):
    core = core_ref[0]
    row = lax.broadcasted_iota(jnp.int32, (HALF, RANK), 0)
    column = lax.broadcasted_iota(jnp.int32, (HALF, RANK), 1)
    diagonal = jnp.where(column == row + core * HALF, half_ref[:, OWN_COLS:], 0.0)
    scale = lax.rsqrt(jnp.sum(diagonal, axis=1, keepdims=True))
    right = half_ref[:, :OWN_COLS] * scale
    mine = pl.ds(pl.multiple_of(core * OWN_ROWS, OWN_ROWS), OWN_ROWS)
    its = pl.ds(pl.multiple_of((1 - core) * OWN_ROWS, OWN_ROWS), OWN_ROWS)
    out_ref[mine, :] = outer_rows_paired(buffer_ref[...], right)
    out_ref[its, :] = outer_rows_paired(other_ref[...], right)


def write_first_factor(sums_ref, inverse_ref):
    gram = sums_ref[:, OWN_COLS:]
    scale, scale_row = scales_of(gram)
    write_inverse_factor(gram * scale * scale_row, inverse_ref, None)


def early_factor_kernel(core_ref, sums_ref, inverse_ref):
    @pl.when(core_ref[0] == 1)
    def _():
        write_first_factor(sums_ref, inverse_ref)


def middle_kernel(core_ref, sums_ref, early_ref, inverse_ref, squares_ref):
    @pl.when(core_ref[0] == 0)
    def _():
        write_first_factor(sums_ref, inverse_ref)

    @pl.when(core_ref[0] == 1)
    def _():
        inverse_ref[...] = early_ref[...]

    scale, _ = scales_of(sums_ref[:, OWN_COLS:])
    right = product(inverse_ref[...], sums_ref[:, :OWN_COLS] * scale)
    squares_ref[...] = as_row(jnp.sum(right * right, axis=1, keepdims=True))


def second_left_kernel(
    core_ref, raw_ref, raw_other_ref, inverse_ref, squares_ref, buffer_ref, other_ref, left_ref, out_ref
):
    first_core = core_ref[0] == 0
    pick = lambda a, b: jnp.where(first_core, a, b)
    mine, its = raw_ref[...], raw_other_ref[...]
    raw = jnp.concatenate([pick(mine, its), pick(its, mine)], axis=1)
    squares = jnp.sum(squares_ref[...], axis=0, keepdims=True)
    left = outer_rows(raw, inverse_ref[...]) / (jnp.sqrt(squares) + norm_eps)
    left_ref[...] = pick(left[:OWN_ROWS], left[OWN_ROWS:])
    turned = pick(left[:, :HALF], left[:, HALF:]).T
    early, late = turned[:, :OWN_ROWS], turned[:, OWN_ROWS:]
    out_ref[:, :OWN_COLS] = product(pick(early, late), buffer_ref[...]) + product(
        pick(late, early), other_ref[...]
    )
    out_ref[:, OWN_COLS:] = product(turned, left)


def last_right_kernel(sums_ref, inverse_ref, right_ref, squares_ref):
    gram = sums_ref[:, OWN_COLS:]
    scale, scale_row = scales_of(gram)
    write_inverse_factor(gram * scale * scale_row, inverse_ref, scale_row)
    right = product(inverse_ref[...], sums_ref[:, :OWN_COLS])
    right_ref[...] = right
    squares = as_row(jnp.sum(right * right, axis=1, keepdims=True))
    squares_ref[...] = jnp.broadcast_to(squares[None], (DP, 1, RANK))


def momentum_kernel(raw_ref, inverse_ref, right_ref, buffer_ref, left_ref, out_ref):
    left = outer_rows(raw_ref[...], inverse_ref[...])
    left_ref[...] = left
    out_ref[...] = buffer_ref[...] - (1.0 - retain) * product_of_parts(left, right_ref[...])


def weight_kernel(
    left_ref, right_ref, squares_ref, weight_ref, basis_out, weight_out, own_b, own_w, done
):
    squares = as_column(jnp.sum(squares_ref[...], axis=0))
    basis = right_ref[...] / (jnp.sqrt(squares) + norm_eps)
    own_b[...] = basis.T
    first = pltpu.make_async_copy(own_b, basis_out, done.at[0])
    first.start()
    update = product_of_parts(left_ref[...], basis)
    own_w[...] = (weight_ref[...].astype(jnp.float32) - step * update).astype(jnp.bfloat16)
    second = pltpu.make_async_copy(own_w, weight_out, done.at[1])
    second.start()
    first.wait()
    second.wait()


def call(kernel, products, *shapes, **options):
    vmem = options.pop("vmem", 24)
    dtypes = options.pop("dtypes", [jnp.float32] * len(shapes))
    out = tuple(jax.ShapeDtypeStruct(s, d) for s, d in zip(shapes, dtypes))
    return pl.pallas_call(
        kernel,
        out_shape=out if len(out) > 1 else out[0],
        cost_estimate=pl.CostEstimate(
            flops=int(products * 12 * RANK * RANK * OWN_COLS),
            bytes_accessed=4 * RANK * OWN_COLS,
            transcendentals=0,
        ),
        compiler_params=pltpu.CompilerParams(vmem_limit_bytes=vmem * 2**20),
        **options,
    )


def scatter_sum(values, axis, count, groups=None):
    rows, columns = values.shape
    parts = lax.all_to_all(values, axis, 0, 0, axis_index_groups=groups, tiled=True)
    return jnp.sum(parts.reshape(count, rows // count, columns), axis=0)


def gather(values, axis, count, groups=None):
    copies = jnp.broadcast_to(values[None], (count,) + values.shape)
    return lax.all_to_all(copies, axis, 0, 0, axis_index_groups=groups, tiled=True)


def sum_over_chips(values):
    own = scatter_sum(values, "mp", MP // 2, SAME_CORE)
    return gather(own, "mp", MP // 2, SAME_CORE).reshape(values.shape)


def with_other_core(values):
    return lax.ppermute(values, "mp", CORE_PAIRS)


def joined(half, first_core):
    other = with_other_core(half)
    return jnp.concatenate(
        [jnp.where(first_core, half, other), jnp.where(first_core, other, half)], axis=0
    )


def body(momentum, gradient, weight, right_basis):
    square = (RANK, RANK)
    wide = (RANK, OWN_COLS)
    width = OWN_COLS + RANK
    block = (OWN_ROWS, OWN_COLS)
    anywhere = pl.BlockSpec(memory_space=pl.ANY)
    scalar = pl.BlockSpec(memory_space=pltpu.SMEM)
    vector = pl.BlockSpec(memory_space=pltpu.VMEM)

    core = (lax.axis_index("mp") % 2).astype(jnp.uint32)
    first_core, own_start, other_start, zero, core, right_basis = lax.optimization_barrier(
        (
            core == 0,
            core * HALF,
            HALF - core * HALF,
            core * 0,
            core.astype(jnp.int32).reshape(1),
            right_basis,
        )
    )

    buffer, left = call(first_kernel, 1, block, (OWN_ROWS, RANK), vmem=60)(
        momentum, gradient, right_basis
    )
    buffer_other = with_other_core(buffer)
    left = gather(scatter_sum(left, "dp", DP), "dp", DP).reshape(OWN_ROWS, RANK)
    sums = call(sums_kernel, 1.3, (RANK, width))(left, buffer)
    half = lax.dynamic_slice(sums, (own_start, zero), (HALF, width))
    other = lax.dynamic_slice(sums, (other_start, zero), (HALF, width))
    half = scatter_sum(half + with_other_core(other), "mp", MP // 2, SAME_CORE)
    half, buffer_other = lax.optimization_barrier((half, buffer_other))
    half = gather(half, "mp", MP // 2, SAME_CORE).reshape(HALF, width)
    raw = call(
        next_left_kernel, 1, (2 * OWN_ROWS, HALF), in_specs=[scalar, vector, vector, vector]
    )(core, half, buffer, buffer_other)
    sums = joined(half, first_core)
    early = call(early_factor_kernel, 1, square, in_specs=[scalar, vector])(core, sums)
    raw, early = lax.optimization_barrier((raw, early))
    raw = scatter_sum(raw, "dp", DP)
    inverse, own_squares = call(
        middle_kernel, 8, square, (1, RANK), in_specs=[scalar, vector, vector]
    )(core, sums, early)
    shared = 2 * OWN_ROWS // DP
    sent = [raw.reshape(shared // 2, 2, HALF), own_squares.reshape(1, 2, HALF)]
    came = gather(jnp.concatenate(sent, axis=0), "dp", DP)
    raw = came[:, : shared // 2].reshape(2 * OWN_ROWS, HALF)
    squares = came[:, shared // 2].reshape(DP, RANK)

    left, half = call(
        second_left_kernel, 1.6, square, (HALF, width), in_specs=[scalar] + [vector] * 6
    )(core, raw, with_other_core(raw), inverse, squares, buffer, buffer_other)
    sums = joined(sum_over_chips(half), first_core)
    inverse, right, own_squares = call(last_right_kernel, 8, square, wide, (DP, 1, RANK))(sums)
    squares = lax.all_to_all(own_squares, "dp", 0, 0, tiled=True)
    left, new_momentum = call(momentum_kernel, 1, square, block)(left, inverse, right, buffer)
    basis, new_weight = call(
        weight_kernel,
        1,
        (OWN_COLS, RANK),
        block,
        dtypes=[jnp.float32, jnp.bfloat16],
        out_specs=(anywhere, anywhere),
        scratch_shapes=[
            pltpu.VMEM((OWN_COLS, RANK), jnp.float32),
            pltpu.VMEM(block, jnp.bfloat16),
            pltpu.SemaphoreType.DMA((2,)),
        ],
    )(left, right, squares, weight)
    return (new_weight, new_momentum, basis)


def solution(mesh):
    in_specs = (P("mp", "dp"), P("mp", "dp"), P("mp", "dp"), P("dp", None))
    out_specs = (P("mp", "dp"), P("mp", "dp"), P("dp", None))
    return jax.shard_map(body, mesh=mesh, in_specs=in_specs, out_specs=out_specs, check_vma=False)
```

```python
import math

import jax
import jax.numpy as jnp
from jax import lax
from jax.experimental import pallas as pl
from jax.experimental.pallas import tpu as pltpu
from jax.sharding import PartitionSpec as P

ROWS = 8192
COLS = 14336
RANK = 256
ITERS = 2

highest = lax.Precision.HIGHEST
retain = 0.95
step_size = 0.5
norm_eps = 1e-06
step = step_size * math.sqrt(ROWS * COLS / RANK)

MP = 32
DP = 16
HALF = RANK // 2
PANEL = 16
PARTS = COLS // DP // HALF
OWN_ROWS = ROWS // MP
OWN_COLS = COLS // DP
SAME_CORE = [[c + 2 * i for i in range(MP // 2)] for c in range(2)]
CORE_PAIRS = [(i, i ^ 1) for i in range(MP)]
NEXT_TO = (((1,), (1,)), ((), ()))


def product(first, second):
    return jnp.dot(first, second, precision=highest, preferred_element_type=jnp.float32)


def outer_rows(first, second):
    return lax.dot_general(
        first, second, NEXT_TO, precision=highest, preferred_element_type=jnp.float32
    )


def two_parts(values):
    high = values.astype(jnp.bfloat16)
    return high, (values - high.astype(jnp.float32)).astype(jnp.bfloat16)


def three_parts(values):
    high = values.astype(jnp.bfloat16)
    rest = values - high.astype(jnp.float32)
    middle = rest.astype(jnp.bfloat16)
    return high, middle, (rest - middle.astype(jnp.float32)).astype(jnp.bfloat16)


def product_of_parts(first, second):
    high, low = two_parts(first)
    other_high, other_low = two_parts(second)
    dot = lambda a, b: jnp.dot(a, b, preferred_element_type=jnp.float32)
    return dot(high, other_high) + (dot(high, other_low) + dot(low, other_high))


def outer_rows_paired(first, second):
    rows = second.shape[0]
    a, b, c = three_parts(first)
    high, middle, low = three_parts(second)
    dot = lambda x, y: lax.dot_general(x, y, NEXT_TO, preferred_element_type=jnp.float32)
    pair = jnp.concatenate([high, middle], axis=0)
    by_a, by_b = dot(a, pair), dot(b, pair)
    small = by_b[:, rows:] + dot(a, low) + dot(c, high)
    return by_a[:, :rows] + (by_a[:, rows:] + by_b[:, :rows] + small)


def on_diagonal():
    row = lax.broadcasted_iota(jnp.int32, (RANK, RANK), 0)
    return row == lax.broadcasted_iota(jnp.int32, (RANK, RANK), 1)


def as_row(column):
    return jnp.sum(jnp.where(on_diagonal(), column, 0.0), axis=0, keepdims=True)


def as_column(row):
    return jnp.sum(jnp.where(on_diagonal(), row, 0.0), axis=1, keepdims=True)


def scales_of(gram):
    diagonal = jnp.where(on_diagonal(), gram, 0.0)
    return (
        lax.rsqrt(jnp.sum(diagonal, axis=1, keepdims=True)),
        lax.rsqrt(jnp.sum(diagonal, axis=0, keepdims=True)),
    )


def spread(row):
    return jnp.broadcast_to(row, (8, HALF))


def doubled(values):
    return jnp.concatenate([values, values], axis=1)


def write_inverse_factor(rest, out_ref, unscale):
    lane = lax.broadcasted_iota(jnp.int32, (PANEL, RANK), 1)
    place = lax.broadcasted_iota(jnp.int32, (PANEL, RANK), 0)
    short = lax.broadcasted_iota(jnp.int32, (8, HALF), 0)
    groups = PANEL // 8
    panel, rest = rest[:PANEL], rest[PANEL:]
    for start in range(0, RANK, PANEL):
        own = [
            {
                g: jnp.broadcast_to(
                    panel[8 * g : 8 * g + 8, start + t : start + t + 1], (8, HALF)
                )
                for g in range(t // 8, groups)
            }
            for t in range(PANEL)
        ]
        inside = (lane >= start) & (lane < start + PANEL)
        panel = jnp.where(inside, jnp.where(lane - start == place, 1.0, 0.0), panel)
        rows = [panel[8 * g : 8 * g + 8] for g in range(groups)]
        pivots = [None] * groups
        for t in range(0, PANEL, 2):
            at, row = divmod(t, 8)
            one, two = own[t], own[t + 1]
            p = spread(one[at][row : row + 1])
            r = spread(one[at][row + 1 : row + 2])
            minor = p * spread(two[at][row + 1 : row + 2]) - r * r
            over_p = 1.0 / p
            over_q = p * (1.0 / minor)
            ratio = r * over_p
            pair = jnp.where(short == row, p, minor * over_p)
            pivots[at] = jnp.where(short >= row, pair, pivots[at]) if row else pair
            two = {g: two[g] - one[g] * ratio for g in range(at, groups)}
            by_one = {g: one[g] * over_p for g in range(at, groups)}
            by_two = {g: two[g] * over_q for g in range(at, groups)}
            by_one[at] = jnp.where(short > row, by_one[at], 0.0)
            by_two[at] = jnp.where(short > row + 1, by_two[at], 0.0)
            for later in range(t + 2, PANEL):
                its_group, its_row = divmod(later, 8)
                from_one = spread(one[its_group][its_row : its_row + 1])
                from_two = spread(two[its_group][its_row : its_row + 1])
                for g in range(its_group, groups):
                    own[later][g] = own[later][g] - by_one[g] * from_one - by_two[g] * from_two
            first = rows[at][row : row + 1]
            second = rows[at][row + 1 : row + 2] - doubled(ratio[:1]) * first
            for g in range(at, groups):
                rows[g] = rows[g] - doubled(by_one[g]) * first - doubled(by_two[g]) * second
        for g in range(groups):
            root = lax.rsqrt(pivots[g])
            rows[g] = rows[g] * doubled(root)
        done = jnp.concatenate(rows, axis=0)
        result = jnp.where(lane < start + PANEL, done, 0.0)
        out_ref[start : start + PANEL, :] = result if unscale is None else result * unscale
        end = start + PANEL
        if end < RANK:
            a, b, c = three_parts(done)
            first = jnp.concatenate([a, a, b, b, a, c], axis=0)
            second = jnp.concatenate([a, b, a, b, c, a], axis=0)
            base = 0 if end < HALF else HALF
            taken = lax.dot_general(
                first[:, base:],
                second,
                (((0,), (0,)), ((), ())),
                preferred_element_type=jnp.float32,
            )
            kept = jnp.where(inside, 0.0, 1.0)[:1]
            at = end - base
            panel = rest[:PANEL] * kept - taken[at : at + PANEL]
            if end + PANEL < RANK:
                rest = rest[PANEL:] * kept - taken[at + PANEL :]


def first_kernel(momentum_ref, gradient_ref, basis_ref, buffer_ref, left_ref):
    buffer = momentum_ref[...] + gradient_ref[...].astype(jnp.float32)
    buffer_ref[...] = buffer
    left_ref[...] = product(buffer, basis_ref[...])


def sums_kernel(left_ref, buffer_ref, out_ref):
    left = left_ref[...]
    turned = left.T
    out_ref[:, :OWN_COLS] = product(turned, buffer_ref[...])
    out_ref[:, OWN_COLS:] = product(turned, left)


def next_left_kernel(core_ref, half_ref, buffer_ref, other_ref, out_ref):
    core = core_ref[0]
    row = lax.broadcasted_iota(jnp.int32, (HALF, RANK), 0)
    column = lax.broadcasted_iota(jnp.int32, (HALF, RANK), 1)
    diagonal = jnp.where(column == row + core * HALF, half_ref[:, OWN_COLS:], 0.0)
    scale = lax.rsqrt(jnp.sum(diagonal, axis=1, keepdims=True))
    right = half_ref[:, :OWN_COLS] * scale
    mine = pl.ds(pl.multiple_of(core * OWN_ROWS, OWN_ROWS), OWN_ROWS)
    its = pl.ds(pl.multiple_of((1 - core) * OWN_ROWS, OWN_ROWS), OWN_ROWS)
    out_ref[mine, :] = outer_rows_paired(buffer_ref[...], right)
    out_ref[its, :] = outer_rows_paired(other_ref[...], right)


def both_halves(core_ref, half_ref, other_ref):
    first_core = core_ref[0] == 0
    half, other = half_ref[...], other_ref[...]
    return jnp.concatenate(
        [jnp.where(first_core, half, other), jnp.where(first_core, other, half)], axis=0
    )


def write_first_factor(sums, inverse_ref):
    gram = sums[:, OWN_COLS:]
    scale, scale_row = scales_of(gram)
    write_inverse_factor(gram * scale * scale_row, inverse_ref, None)


def early_factor_kernel(core_ref, half_ref, other_ref, inverse_ref):
    @pl.when(core_ref[0] == 1)
    def _():
        write_first_factor(both_halves(core_ref, half_ref, other_ref), inverse_ref)


def middle_kernel(core_ref, half_ref, other_ref, early_ref, inverse_ref, squares_ref):
    sums = both_halves(core_ref, half_ref, other_ref)

    @pl.when(core_ref[0] == 0)
    def _():
        write_first_factor(sums, inverse_ref)

    @pl.when(core_ref[0] == 1)
    def _():
        inverse_ref[...] = early_ref[...]

    scale, _ = scales_of(sums[:, OWN_COLS:])
    right = product(inverse_ref[...], sums[:, :OWN_COLS] * scale)
    squares_ref[...] = as_row(jnp.sum(right * right, axis=1, keepdims=True))


def second_left_kernel(
    core_ref, raw_ref, raw_other_ref, inverse_ref, squares_ref, buffer_ref, other_ref, left_ref, out_ref
):
    first_core = core_ref[0] == 0
    pick = lambda a, b: jnp.where(first_core, a, b)
    mine, its = raw_ref[...], raw_other_ref[...]
    raw = jnp.concatenate([pick(mine, its), pick(its, mine)], axis=1)
    squares = jnp.sum(squares_ref[...], axis=0, keepdims=True)
    left = outer_rows(raw, inverse_ref[...]) / (jnp.sqrt(squares) + norm_eps)
    left_ref[...] = pick(left[:OWN_ROWS], left[OWN_ROWS:])
    turned = pick(left[:, :HALF], left[:, HALF:]).T
    early, late = turned[:, :OWN_ROWS], turned[:, OWN_ROWS:]
    out_ref[:, :OWN_COLS] = product(pick(early, late), buffer_ref[...]) + product(
        pick(late, early), other_ref[...]
    )
    out_ref[:, OWN_COLS:] = product(turned, left)


def last_right_kernel(core_ref, half_ref, other_ref, inverse_ref, right_ref, squares_ref):
    sums = both_halves(core_ref, half_ref, other_ref)
    gram = sums[:, OWN_COLS:]
    scale, scale_row = scales_of(gram)
    write_inverse_factor(gram * scale * scale_row, inverse_ref, scale_row)
    right = product(inverse_ref[...], sums[:, :OWN_COLS])
    right_ref[...] = right
    squares = as_row(jnp.sum(right * right, axis=1, keepdims=True))
    squares_ref[...] = jnp.broadcast_to(squares[None], (DP, 1, RANK))


def momentum_kernel(raw_ref, inverse_ref, right_ref, buffer_ref, left_ref, out_ref):
    left = outer_rows(raw_ref[...], inverse_ref[...])
    left_ref[...] = left
    out_ref[...] = buffer_ref[...] - (1.0 - retain) * product_of_parts(left, right_ref[...])


def weight_kernel(
    left_ref, right_ref, squares_ref, weight_ref, basis_out, weight_out, own_b, own_w, done
):
    squares = as_column(jnp.sum(squares_ref[...], axis=0))
    basis = right_ref[...] / (jnp.sqrt(squares) + norm_eps)
    copies = []
    for j in range(PARTS):
        at = pl.ds(j * HALF, HALF)
        own_b[at, :] = basis[:, j * HALF : (j + 1) * HALF].T
        copies.append(pltpu.make_async_copy(own_b.at[at, :], basis_out.at[at, :], done.at[j]))
        copies[-1].start()
    update = product_of_parts(left_ref[...], basis)
    own_w[...] = (weight_ref[...].astype(jnp.float32) - step * update).astype(jnp.bfloat16)
    copies.append(pltpu.make_async_copy(own_w, weight_out, done.at[PARTS]))
    copies[-1].start()
    for copy in copies:
        copy.wait()


def call(kernel, products, *shapes, **options):
    vmem = options.pop("vmem", 24)
    dtypes = options.pop("dtypes", [jnp.float32] * len(shapes))
    out = tuple(jax.ShapeDtypeStruct(s, d) for s, d in zip(shapes, dtypes))
    return pl.pallas_call(
        kernel,
        out_shape=out if len(out) > 1 else out[0],
        cost_estimate=pl.CostEstimate(
            flops=int(products * 12 * RANK * RANK * OWN_COLS),
            bytes_accessed=4 * RANK * OWN_COLS,
            transcendentals=0,
        ),
        compiler_params=pltpu.CompilerParams(vmem_limit_bytes=vmem * 2**20),
        **options,
    )


def scatter_sum(values, axis, count, groups=None):
    rows, columns = values.shape
    parts = lax.all_to_all(values, axis, 0, 0, axis_index_groups=groups, tiled=True)
    return jnp.sum(parts.reshape(count, rows // count, columns), axis=0)


def gather(values, axis, count, groups=None):
    copies = jnp.broadcast_to(values[None], (count,) + values.shape)
    return lax.all_to_all(copies, axis, 0, 0, axis_index_groups=groups, tiled=True)


def sum_over_chips(values):
    own = scatter_sum(values, "mp", MP // 2, SAME_CORE)
    return gather(own, "mp", MP // 2, SAME_CORE).reshape(values.shape)


def with_other_core(values):
    return lax.ppermute(values, "mp", CORE_PAIRS)


def body(momentum, gradient, weight, right_basis):
    square = (RANK, RANK)
    wide = (RANK, OWN_COLS)
    width = OWN_COLS + RANK
    block = (OWN_ROWS, OWN_COLS)
    anywhere = pl.BlockSpec(memory_space=pl.ANY)
    scalar = pl.BlockSpec(memory_space=pltpu.SMEM)
    vector = pl.BlockSpec(memory_space=pltpu.VMEM)

    core = (lax.axis_index("mp") % 2).astype(jnp.uint32)
    own_start, other_start, zero, core, right_basis = lax.optimization_barrier(
        (
            core * HALF,
            HALF - core * HALF,
            core * 0,
            core.astype(jnp.int32).reshape(1),
            right_basis,
        )
    )

    buffer, left = call(first_kernel, 1, block, (OWN_ROWS, RANK), vmem=60)(
        momentum, gradient, right_basis
    )
    buffer_other = with_other_core(buffer)
    left = gather(scatter_sum(left, "dp", DP), "dp", DP).reshape(OWN_ROWS, RANK)
    sums = call(sums_kernel, 1.3, (RANK, width))(left, buffer)
    half = lax.dynamic_slice(sums, (own_start, zero), (HALF, width))
    other = lax.dynamic_slice(sums, (other_start, zero), (HALF, width))
    half = scatter_sum(half + with_other_core(other), "mp", MP // 2, SAME_CORE)
    half, buffer_other = lax.optimization_barrier((half, buffer_other))
    half = gather(half, "mp", MP // 2, SAME_CORE).reshape(HALF, width)
    raw = call(
        next_left_kernel, 1, (2 * OWN_ROWS, HALF), in_specs=[scalar, vector, vector, vector]
    )(core, half, buffer, buffer_other)
    halves = (core, half, with_other_core(half))
    early = call(early_factor_kernel, 1, square, in_specs=[scalar, vector, vector])(*halves)
    raw, early = lax.optimization_barrier((raw, early))
    raw = scatter_sum(raw, "dp", DP)
    inverse, own_squares = call(
        middle_kernel, 8, square, (1, RANK), in_specs=[scalar] + [vector] * 3
    )(*halves, early)
    shared = 2 * OWN_ROWS // DP
    sent = [raw.reshape(shared // 2, 2, HALF), own_squares.reshape(1, 2, HALF)]
    came = gather(jnp.concatenate(sent, axis=0), "dp", DP)
    raw = came[:, : shared // 2].reshape(2 * OWN_ROWS, HALF)
    squares = came[:, shared // 2].reshape(DP, RANK)

    left, half = call(
        second_left_kernel, 1.6, square, (HALF, width), in_specs=[scalar] + [vector] * 6
    )(core, raw, with_other_core(raw), inverse, squares, buffer, buffer_other)
    half = sum_over_chips(half)
    inverse, right, own_squares = call(
        last_right_kernel,
        8,
        square,
        wide,
        (DP, 1, RANK),
        in_specs=[scalar, vector, vector],
    )(core, half, with_other_core(half))
    squares = lax.all_to_all(own_squares, "dp", 0, 0, tiled=True)
    left, new_momentum = call(momentum_kernel, 1, square, block)(left, inverse, right, buffer)
    basis, new_weight = call(
        weight_kernel,
        1,
        (OWN_COLS, RANK),
        block,
        dtypes=[jnp.float32, jnp.bfloat16],
        out_specs=(anywhere, anywhere),
        scratch_shapes=[
            pltpu.VMEM((OWN_COLS, RANK), jnp.float32),
            pltpu.VMEM(block, jnp.bfloat16),
            pltpu.SemaphoreType.DMA((PARTS + 1,)),
        ],
    )(left, right, squares, weight)
    return (new_weight, new_momentum, basis)


def solution(mesh):
    in_specs = (P("mp", "dp"), P("mp", "dp"), P("mp", "dp"), P("dp", None))
    out_specs = (P("mp", "dp"), P("mp", "dp"), P("dp", None))
    return jax.shard_map(body, mesh=mesh, in_specs=in_specs, out_specs=out_specs, check_vma=False)
```

```python
import math

import jax
import jax.numpy as jnp
from jax import lax
from jax.experimental import pallas as pl
from jax.experimental.pallas import tpu as pltpu
from jax.sharding import PartitionSpec as P

ROWS = 8192
COLS = 14336
RANK = 256
ITERS = 2

highest = lax.Precision.HIGHEST
retain = 0.95
step_size = 0.5
norm_eps = 1e-06
step = step_size * math.sqrt(ROWS * COLS / RANK)

MP = 32
DP = 16
HALF = RANK // 2
PANEL = 16
PARTS = COLS // DP // HALF
OWN_ROWS = ROWS // MP
OWN_COLS = COLS // DP
SAME_CORE = [[c + 2 * i for i in range(MP // 2)] for c in range(2)]
CORE_PAIRS = [(i, i ^ 1) for i in range(MP)]
NEXT_TO = (((1,), (1,)), ((), ()))


def product(first, second):
    return jnp.dot(first, second, precision=highest, preferred_element_type=jnp.float32)


def outer_rows(first, second):
    return lax.dot_general(
        first, second, NEXT_TO, precision=highest, preferred_element_type=jnp.float32
    )


def two_parts(values):
    high = values.astype(jnp.bfloat16)
    return high, (values - high.astype(jnp.float32)).astype(jnp.bfloat16)


def three_parts(values):
    high = values.astype(jnp.bfloat16)
    rest = values - high.astype(jnp.float32)
    middle = rest.astype(jnp.bfloat16)
    return high, middle, (rest - middle.astype(jnp.float32)).astype(jnp.bfloat16)


def product_of_parts(first, second):
    high, low = two_parts(first)
    other_high, other_low = two_parts(second)
    dot = lambda a, b: jnp.dot(a, b, preferred_element_type=jnp.float32)
    return dot(high, other_high) + (dot(high, other_low) + dot(low, other_high))


def outer_rows_paired(first, second):
    rows = second.shape[0]
    a, b, c = three_parts(first)
    high, middle, low = three_parts(second)
    dot = lambda x, y: lax.dot_general(x, y, NEXT_TO, preferred_element_type=jnp.float32)
    pair = jnp.concatenate([high, middle], axis=0)
    by_a, by_b = dot(a, pair), dot(b, pair)
    small = by_b[:, rows:] + dot(a, low) + dot(c, high)
    return by_a[:, :rows] + (by_a[:, rows:] + by_b[:, :rows] + small)


def on_diagonal():
    row = lax.broadcasted_iota(jnp.int32, (RANK, RANK), 0)
    return row == lax.broadcasted_iota(jnp.int32, (RANK, RANK), 1)


def as_row(column):
    return jnp.sum(jnp.where(on_diagonal(), column, 0.0), axis=0, keepdims=True)


def as_column(row):
    return jnp.sum(jnp.where(on_diagonal(), row, 0.0), axis=1, keepdims=True)


def scales_of(gram):
    diagonal = jnp.where(on_diagonal(), gram, 0.0)
    return (
        lax.rsqrt(jnp.sum(diagonal, axis=1, keepdims=True)),
        lax.rsqrt(jnp.sum(diagonal, axis=0, keepdims=True)),
    )


def spread(row):
    return jnp.broadcast_to(row, (8, HALF))


def doubled(values):
    return jnp.concatenate([values, values], axis=1)


def write_inverse_factor(rest, out_ref, unscale):
    lane = lax.broadcasted_iota(jnp.int32, (PANEL, RANK), 1)
    place = lax.broadcasted_iota(jnp.int32, (PANEL, RANK), 0)
    short = lax.broadcasted_iota(jnp.int32, (8, HALF), 0)
    groups = PANEL // 8
    panel, rest = rest[:PANEL], rest[PANEL:]
    for start in range(0, RANK, PANEL):
        own = [
            {
                g: jnp.broadcast_to(
                    panel[8 * g : 8 * g + 8, start + t : start + t + 1], (8, HALF)
                )
                for g in range(t // 8, groups)
            }
            for t in range(PANEL)
        ]
        inside = (lane >= start) & (lane < start + PANEL)
        panel = jnp.where(inside, jnp.where(lane - start == place, 1.0, 0.0), panel)
        rows = [panel[8 * g : 8 * g + 8] for g in range(groups)]
        pivots = [None] * groups
        for t in range(0, PANEL, 2):
            at, row = divmod(t, 8)
            one, two = own[t], own[t + 1]
            p = spread(one[at][row : row + 1])
            r = spread(one[at][row + 1 : row + 2])
            minor = p * spread(two[at][row + 1 : row + 2]) - r * r
            over_p = 1.0 / p
            over_q = p * (1.0 / minor)
            ratio = r * over_p
            pair = jnp.where(short == row, p, minor * over_p)
            pivots[at] = jnp.where(short >= row, pair, pivots[at]) if row else pair
            two = {g: two[g] - one[g] * ratio for g in range(at, groups)}
            by_one = {g: one[g] * over_p for g in range(at, groups)}
            by_two = {g: two[g] * over_q for g in range(at, groups)}
            by_one[at] = jnp.where(short > row, by_one[at], 0.0)
            by_two[at] = jnp.where(short > row + 1, by_two[at], 0.0)
            for later in range(t + 2, PANEL):
                its_group, its_row = divmod(later, 8)
                from_one = spread(one[its_group][its_row : its_row + 1])
                from_two = spread(two[its_group][its_row : its_row + 1])
                for g in range(its_group, groups):
                    own[later][g] = own[later][g] - by_one[g] * from_one - by_two[g] * from_two
            first = rows[at][row : row + 1]
            second = rows[at][row + 1 : row + 2] - doubled(ratio[:1]) * first
            for g in range(at, groups):
                rows[g] = rows[g] - doubled(by_one[g]) * first - doubled(by_two[g]) * second
        for g in range(groups):
            root = lax.rsqrt(pivots[g])
            rows[g] = rows[g] * doubled(root)
        done = jnp.concatenate(rows, axis=0)
        result = jnp.where(lane < start + PANEL, done, 0.0)
        out_ref[start : start + PANEL, :] = result if unscale is None else result * unscale
        end = start + PANEL
        if end < RANK:
            a, b, c = three_parts(done)
            first = jnp.concatenate([a, a, b, b, a, c], axis=0)
            second = jnp.concatenate([a, b, a, b, c, a], axis=0)
            base = 0 if end < HALF else HALF
            taken = lax.dot_general(
                first[:, base:],
                second,
                (((0,), (0,)), ((), ())),
                preferred_element_type=jnp.float32,
            )
            kept = jnp.where(inside, 0.0, 1.0)[:1]
            at = end - base
            panel = rest[:PANEL] * kept - taken[at : at + PANEL]
            if end + PANEL < RANK:
                rest = rest[PANEL:] * kept - taken[at + PANEL :]


def first_kernel(momentum_ref, gradient_ref, basis_ref, buffer_ref, left_ref):
    buffer = momentum_ref[...] + gradient_ref[...].astype(jnp.float32)
    buffer_ref[...] = buffer
    left_ref[...] = product(buffer, basis_ref[...])


def sums_kernel(core_ref, left_ref, buffer_ref, own_ref, other_ref):
    first_core = core_ref[0] == 0
    left = left_ref[...]
    turned = left.T
    for at, right in ((0, buffer_ref[...]), (OWN_COLS, left)):
        columns = slice(at, at + right.shape[1])
        sums = product(turned, right)
        own_ref[:, columns] = jnp.where(first_core, sums[:HALF], sums[HALF:])
        other_ref[:, columns] = jnp.where(first_core, sums[HALF:], sums[:HALF])


def next_left_kernel(core_ref, half_ref, buffer_ref, other_ref, out_ref):
    core = core_ref[0]
    row = lax.broadcasted_iota(jnp.int32, (HALF, RANK), 0)
    column = lax.broadcasted_iota(jnp.int32, (HALF, RANK), 1)
    diagonal = jnp.where(column == row + core * HALF, half_ref[:, OWN_COLS:], 0.0)
    scale = lax.rsqrt(jnp.sum(diagonal, axis=1, keepdims=True))
    right = half_ref[:, :OWN_COLS] * scale
    mine = pl.ds(pl.multiple_of(core * OWN_ROWS, OWN_ROWS), OWN_ROWS)
    its = pl.ds(pl.multiple_of((1 - core) * OWN_ROWS, OWN_ROWS), OWN_ROWS)
    out_ref[mine, :] = outer_rows_paired(buffer_ref[...], right)
    out_ref[its, :] = outer_rows_paired(other_ref[...], right)


def both_halves(core_ref, half_ref, other_ref):
    first_core = core_ref[0] == 0
    half, other = half_ref[...], other_ref[...]
    return jnp.concatenate(
        [jnp.where(first_core, half, other), jnp.where(first_core, other, half)], axis=0
    )


def write_first_factor(sums, inverse_ref):
    gram = sums[:, OWN_COLS:]
    scale, scale_row = scales_of(gram)
    write_inverse_factor(gram * scale * scale_row, inverse_ref, None)


def early_factor_kernel(core_ref, half_ref, other_ref, inverse_ref):
    @pl.when(core_ref[0] == 1)
    def _():
        write_first_factor(both_halves(core_ref, half_ref, other_ref), inverse_ref)


def middle_kernel(core_ref, half_ref, other_ref, early_ref, inverse_ref, squares_ref):
    sums = both_halves(core_ref, half_ref, other_ref)

    @pl.when(core_ref[0] == 0)
    def _():
        write_first_factor(sums, inverse_ref)

    @pl.when(core_ref[0] == 1)
    def _():
        inverse_ref[...] = early_ref[...]

    scale, _ = scales_of(sums[:, OWN_COLS:])
    right = product(inverse_ref[...], sums[:, :OWN_COLS] * scale)
    squares_ref[...] = as_row(jnp.sum(right * right, axis=1, keepdims=True))


def second_left_kernel(
    core_ref, raw_ref, raw_other_ref, inverse_ref, squares_ref, buffer_ref, other_ref, left_ref, out_ref
):
    first_core = core_ref[0] == 0
    pick = lambda a, b: jnp.where(first_core, a, b)
    mine, its = raw_ref[...], raw_other_ref[...]
    raw = jnp.concatenate([pick(mine, its), pick(its, mine)], axis=1)
    squares = jnp.sum(squares_ref[...], axis=0, keepdims=True)
    norms = as_column(jnp.sqrt(squares) + norm_eps)
    left = outer_rows(raw, inverse_ref[...] / norms)
    left_ref[...] = pick(left[:OWN_ROWS], left[OWN_ROWS:])
    turned = pick(left[:, :HALF], left[:, HALF:]).T
    early, late = turned[:, :OWN_ROWS], turned[:, OWN_ROWS:]
    out_ref[:, :OWN_COLS] = product(pick(early, late), buffer_ref[...]) + product(
        pick(late, early), other_ref[...]
    )
    out_ref[:, OWN_COLS:] = product(turned, left)


def last_right_kernel(core_ref, half_ref, other_ref, inverse_ref, right_ref, squares_ref):
    sums = both_halves(core_ref, half_ref, other_ref)
    gram = sums[:, OWN_COLS:]
    scale, scale_row = scales_of(gram)
    write_inverse_factor(gram * scale * scale_row, inverse_ref, scale_row)
    right = product(inverse_ref[...], sums[:, :OWN_COLS])
    right_ref[...] = right
    squares = as_row(jnp.sum(right * right, axis=1, keepdims=True))
    squares_ref[...] = jnp.broadcast_to(squares[None], (DP, 1, RANK))


def momentum_kernel(raw_ref, inverse_ref, right_ref, buffer_ref, left_ref, out_ref):
    left = outer_rows(raw_ref[...], inverse_ref[...])
    left_ref[...] = left
    out_ref[...] = buffer_ref[...] - (1.0 - retain) * product_of_parts(left, right_ref[...])


def weight_kernel(
    left_ref, right_ref, squares_ref, weight_ref, basis_out, weight_out, own_b, own_w, done
):
    squares = as_column(jnp.sum(squares_ref[...], axis=0))
    basis = right_ref[...] / (jnp.sqrt(squares) + norm_eps)
    copies = []
    for j in range(PARTS):
        at = pl.ds(j * HALF, HALF)
        own_b[at, :] = basis[:, j * HALF : (j + 1) * HALF].T
        copies.append(pltpu.make_async_copy(own_b.at[at, :], basis_out.at[at, :], done.at[j]))
        copies[-1].start()
    update = product_of_parts(left_ref[...], basis)
    own_w[...] = (weight_ref[...].astype(jnp.float32) - step * update).astype(jnp.bfloat16)
    copies.append(pltpu.make_async_copy(own_w, weight_out, done.at[PARTS]))
    copies[-1].start()
    for copy in copies:
        copy.wait()


def call(kernel, products, *shapes, **options):
    vmem = options.pop("vmem", 24)
    dtypes = options.pop("dtypes", [jnp.float32] * len(shapes))
    out = tuple(jax.ShapeDtypeStruct(s, d) for s, d in zip(shapes, dtypes))
    return pl.pallas_call(
        kernel,
        out_shape=out if len(out) > 1 else out[0],
        cost_estimate=pl.CostEstimate(
            flops=int(products * 12 * RANK * RANK * OWN_COLS),
            bytes_accessed=4 * RANK * OWN_COLS,
            transcendentals=0,
        ),
        compiler_params=pltpu.CompilerParams(vmem_limit_bytes=vmem * 2**20),
        **options,
    )


def scatter_sum(values, axis, count, groups=None):
    rows, columns = values.shape
    parts = lax.all_to_all(values, axis, 0, 0, axis_index_groups=groups, tiled=True)
    return jnp.sum(parts.reshape(count, rows // count, columns), axis=0)


def gather(values, axis, count, groups=None):
    copies = jnp.broadcast_to(values[None], (count,) + values.shape)
    return lax.all_to_all(copies, axis, 0, 0, axis_index_groups=groups, tiled=True)


def sum_over_chips(values):
    own = scatter_sum(values, "mp", MP // 2, SAME_CORE)
    return gather(own, "mp", MP // 2, SAME_CORE).reshape(values.shape)


def with_other_core(values):
    return lax.ppermute(values, "mp", CORE_PAIRS)


def body(momentum, gradient, weight, right_basis):
    square = (RANK, RANK)
    wide = (RANK, OWN_COLS)
    width = OWN_COLS + RANK
    block = (OWN_ROWS, OWN_COLS)
    anywhere = pl.BlockSpec(memory_space=pl.ANY)
    scalar = pl.BlockSpec(memory_space=pltpu.SMEM)
    vector = pl.BlockSpec(memory_space=pltpu.VMEM)

    core = (lax.axis_index("mp") % 2).reshape(1)
    core, right_basis = lax.optimization_barrier((core, right_basis))

    buffer, left = call(first_kernel, 1, block, (OWN_ROWS, RANK), vmem=60)(
        momentum, gradient, right_basis
    )
    buffer_other = with_other_core(buffer)
    left = gather(scatter_sum(left, "dp", DP), "dp", DP).reshape(OWN_ROWS, RANK)
    half, other = call(
        sums_kernel, 1.3, (HALF, width), (HALF, width), in_specs=[scalar, vector, vector]
    )(core, left, buffer)
    half = scatter_sum(half + with_other_core(other), "mp", MP // 2, SAME_CORE)
    half, buffer_other = lax.optimization_barrier((half, buffer_other))
    half = gather(half, "mp", MP // 2, SAME_CORE).reshape(HALF, width)
    raw = call(
        next_left_kernel, 1, (2 * OWN_ROWS, HALF), in_specs=[scalar, vector, vector, vector]
    )(core, half, buffer, buffer_other)
    halves = (core, half, with_other_core(half))
    early = call(early_factor_kernel, 1, square, in_specs=[scalar, vector, vector])(*halves)
    raw, early = lax.optimization_barrier((raw, early))
    raw = scatter_sum(raw, "dp", DP)
    inverse, own_squares = call(
        middle_kernel, 8, square, (1, RANK), in_specs=[scalar] + [vector] * 3
    )(*halves, early)
    shared = 2 * OWN_ROWS // DP
    sent = [raw.reshape(shared // 2, 2, HALF), own_squares.reshape(1, 2, HALF)]
    came = gather(jnp.concatenate(sent, axis=0), "dp", DP)
    raw = came[:, : shared // 2].reshape(2 * OWN_ROWS, HALF)
    squares = came[:, shared // 2].reshape(DP, RANK)

    left, half = call(
        second_left_kernel, 1.6, square, (HALF, width), in_specs=[scalar] + [vector] * 6
    )(core, raw, with_other_core(raw), inverse, squares, buffer, buffer_other)
    half = sum_over_chips(half)
    inverse, right, own_squares = call(
        last_right_kernel,
        8,
        square,
        wide,
        (DP, 1, RANK),
        in_specs=[scalar, vector, vector],
    )(core, half, with_other_core(half))
    squares = lax.all_to_all(own_squares, "dp", 0, 0, tiled=True)
    left, new_momentum = call(momentum_kernel, 1, square, block)(left, inverse, right, buffer)
    basis, new_weight = call(
        weight_kernel,
        1,
        (OWN_COLS, RANK),
        block,
        dtypes=[jnp.float32, jnp.bfloat16],
        out_specs=(anywhere, anywhere),
        scratch_shapes=[
            pltpu.VMEM((OWN_COLS, RANK), jnp.float32),
            pltpu.VMEM(block, jnp.bfloat16),
            pltpu.SemaphoreType.DMA((PARTS + 1,)),
        ],
    )(left, right, squares, weight)
    return (new_weight, new_momentum, basis)


def solution(mesh):
    in_specs = (P("mp", "dp"), P("mp", "dp"), P("mp", "dp"), P("dp", None))
    out_specs = (P("mp", "dp"), P("mp", "dp"), P("dp", None))
    return jax.shard_map(body, mesh=mesh, in_specs=in_specs, out_specs=out_specs, check_vma=False)
```
